128 devices in a mesh: gx: 64 (over z, x, y), gy: 2 (over core).
Axes of the slice: x: 4, y: 4, z: 4, core: 2. Of those that a mesh axis runs over, the one named last changes fastest.
Arguments:
- field: bfloat16 [1, 64, 2048, 2048], P(None, None, 'gx', 'gy'), may hold values from -6 to 6
- cotangent: bfloat16 [1, 64, 2048, 2048], P(None, None, 'gx', 'gy'), may hold values from -6 to 6
- local_weight: bfloat16 [64, 64], replicated, may hold values from -0.75 to 0.75
- spectral_weight: bfloat16 [64, 64, 64, 128], P('gx', 'gy'), may hold values from -0.5 to 0.5
Outputs:
- grad_field: bfloat16 [1, 64, 2048, 2048], P(None, None, 'gx', 'gy')
- grad_spectral: float32 [64, 64, 64, 128], P('gx', 'gy')
- grad_local: float32 [64, 64], replicated
The draws below stay inside these ranges and needn't reach their ends.
All inputs are finite; a program needn't handle non-finite values.
Results may differ from the reference program's by a relative error of at most 0.023.
Values may be sent and summed in bfloat16 or wider, within the bound.
No kernel may reach another device: no remote copies, remote signals or barrier semaphores. Data moves between devices by JAX's collectives and lax.ppermute only.
A program may use at most 128 MiB of HBM per device.

```python
import math
import jax
import jax.numpy as jnp
from jax import lax

NX = 2048
NY = 2048
C = 64
MX = 64
MY = 64
PLANES = 1


def block_scale(stream_key, shape, shards, least, high):
    factor_of, own = 1.0, jax.random.fold_in(stream_key, 6)
    for axis_at, parts in shards:
        draws = jnp.exp(jax.random.uniform(jax.random.fold_in(own, axis_at), (parts,), jnp.float32, least / len(shards), high / len(shards)))
        factor_of = factor_of * jnp.repeat(draws, shape[axis_at] // parts).reshape([-1 if axis == axis_at else 1 for axis in range(len(shape))])
    return factor_of


def centred(key, shape, deviation, most, cuts=(), kind=jnp.bfloat16):
    entries = jax.random.normal(key, shape, jnp.float32) * deviation
    if len(cuts) > 0:
        entries = block_scale(key, shape, cuts, -0.22, 0.18) * entries
    return jnp.clip(entries, min=-most, max=most).astype(kind)


def setup_inputs(seed: int = 0) -> dict:
    streams_of = jax.random.split(jax.random.key(seed), 5)
    field = centred(streams_of[0], (PLANES, C, NX, NY), 1.0, 6.0, ((2, 64), (3, 2)))
    cotangent = centred(streams_of[1], (PLANES, C, NX, NY), 1.0, 6.0, ((2, 64), (3, 2)))
    local_weight = centred(streams_of[2], (C, C), C ** -0.5, 0.75)
    spectral_weight = centred(streams_of[3], (MX, MY, C, 2 * C), (2 * C) ** -0.5, 0.5, ((0, 64), (1, 2)))
    return {"field": field, "cotangent": cotangent, "local_weight": local_weight, "spectral_weight": spectral_weight}


TWO_PI = 2.0 * math.pi
ROOT_HALF = 1.0 / math.sqrt(2.0)
ROOT_TWO_PI = 1.0 / math.sqrt(2.0 * math.pi)
EXACT = lax.Precision.HIGHEST

def gelu_slope(values):
    return 0.5 * (1.0 + jax.scipy.special.erf(values * ROOT_HALF)) + values * jnp.exp(-0.5 * values * values) * ROOT_TWO_PI

def phase_pair(frequency, coords, extent):
    residue = frequency[..., None] * coords % extent
    angles = residue.astype(jnp.float32) * (TWO_PI / extent)
    return (jnp.cos(angles), jnp.sin(angles))

def ytable_rows(offset, number):
    coords = offset + jnp.arange(number, dtype=jnp.int32)
    cosine_part, sine_part = phase_pair(jnp.arange(MY, dtype=jnp.int32), coords, NY)
    return jnp.concatenate([cosine_part.T, -sine_part.T], axis=1).astype(jnp.bfloat16)

def x_transform(yparts, cosine_part, sine_part, scale):
    real_in = yparts[..., :MY]
    imag_in = yparts[..., MY:]
    pattern = 'mx,pcxn->pmnc'
    real_out = jnp.einsum(pattern, cosine_part, real_in, precision=EXACT) + jnp.einsum(pattern, sine_part, imag_in, precision=EXACT)
    imag_out = jnp.einsum(pattern, cosine_part, imag_in, precision=EXACT) - jnp.einsum(pattern, sine_part, real_in, precision=EXACT)
    return scale * jnp.concatenate([real_out, imag_out], axis=-1)

def x_inverse(spectrum, cosine_part, sine_part):
    real_in = spectrum[..., :C]
    imag_in = spectrum[..., C:]
    pattern = 'mx,pmnc->pcxn'
    real_out = jnp.einsum(pattern, cosine_part, real_in, precision=EXACT) - jnp.einsum(pattern, sine_part, imag_in, precision=EXACT)
    imag_out = jnp.einsum(pattern, cosine_part, imag_in, precision=EXACT) + jnp.einsum(pattern, sine_part, real_in, precision=EXACT)
    return jnp.concatenate([real_out, imag_out], axis=-1)

def reference(field, cotangent, local_weight, spectral_weight):
    block_rows = math.gcd(NX, 128)
    block_count = NX // block_rows
    forward_scale = 1.0 / math.sqrt(NX * NY)
    inverse_scale = 1.0 / math.sqrt(MX * MY)
    ytable = ytable_rows(0, NY)
    yinverse = ytable.T
    mode_ids = jnp.arange(MX, dtype=jnp.int32)
    frequency = jnp.where(mode_ids < MX // 2, mode_ids, mode_ids + NX - MX)
    block_ids = jnp.arange(block_count, dtype=jnp.int32)
    weights = spectral_weight.astype(jnp.float32)
    local_f = local_weight.astype(jnp.float32)

    def rows_of(array, block_id):
        return lax.dynamic_slice_in_dim(array, block_id * block_rows, block_rows, 2)

    def x_phase(block_id):
        coords = block_id * block_rows + jnp.arange(block_rows, dtype=jnp.int32)
        return phase_pair(frequency, coords, NX)

    def pass_one(running, block_id):
        yparts = jnp.dot(rows_of(field, block_id), ytable, preferred_element_type=jnp.float32)
        cosine_part, sine_part = x_phase(block_id)
        return (running + x_transform(yparts, cosine_part, sine_part, forward_scale), None)
    spectrum, _ = lax.scan(pass_one, jnp.zeros((PLANES, MX, MY, 2 * C), jnp.float32), block_ids)
    spectrum_b = spectrum.astype(jnp.bfloat16)
    real_in = spectrum_b[..., :C].astype(jnp.float32)
    imag_in = spectrum_b[..., C:].astype(jnp.float32)
    from_real = jnp.einsum('pmnc,mnco->pmno', real_in, weights, precision=EXACT)
    from_imag = jnp.einsum('pmnc,mnco->pmno', imag_in, weights, precision=EXACT)
    mixed = jnp.concatenate([from_real[..., :C] - from_imag[..., C:], from_real[..., C:] + from_imag[..., :C]], axis=-1).astype(jnp.bfloat16)
    mixed_f = mixed.astype(jnp.float32)

    def pass_two(carry, block_id):
        weight_sum, grad_sum = carry
        cosine_part, sine_part = x_phase(block_id)
        inner_fwd = x_inverse(mixed_f, cosine_part, sine_part).astype(jnp.bfloat16)
        spatial = inverse_scale * jnp.dot(inner_fwd, yinverse, preferred_element_type=jnp.float32)
        field_rows = rows_of(field, block_id).astype(jnp.float32)
        pre_act = spatial + jnp.einsum('pcxy,co->poxy', field_rows, local_f, precision=EXACT)
        slope_grad = (rows_of(cotangent, block_id).astype(jnp.float32) * gelu_slope(pre_act)).astype(jnp.bfloat16)
        weight_sum = weight_sum + jnp.einsum('pcxy,poxy->co', field_rows, slope_grad.astype(jnp.float32), precision=EXACT)
        yparts = jnp.dot(slope_grad, ytable, preferred_element_type=jnp.float32)
        grad_sum = grad_sum + x_transform(yparts, cosine_part, sine_part, inverse_scale)
        return ((weight_sum, grad_sum), slope_grad)
    start_carry = (jnp.zeros((C, C), jnp.float32), jnp.zeros((PLANES, MX, MY, 2 * C), jnp.float32))
    (weight_sum, grad_sum), slope_blocks = lax.scan(pass_two, start_carry, block_ids)
    grad_local = weight_sum / math.sqrt(PLANES * NX * NY)
    mode_grad = grad_sum.astype(jnp.bfloat16)
    grad_real = mode_grad[..., :C].astype(jnp.float32)
    grad_imag = mode_grad[..., C:].astype(jnp.float32)
    left_pair = jnp.concatenate([grad_real, grad_imag], axis=-1)
    right_pair = jnp.concatenate([grad_imag, -grad_real], axis=-1)
    gamma = math.sqrt(MX * MY / (PLANES * NX * NY))
    grad_spectral = gamma * (jnp.einsum('pmnc,pmno->mnco', real_in, left_pair, precision=EXACT) + jnp.einsum('pmnc,pmno->mnco', imag_in, right_pair, precision=EXACT))
    input_modes = jnp.concatenate([jnp.einsum('pmno,mnco->pmnc', left_pair, weights, precision=EXACT), jnp.einsum('pmno,mnco->pmnc', right_pair, weights, precision=EXACT)], axis=-1).astype(jnp.bfloat16)
    input_f = input_modes.astype(jnp.float32)

    def pass_three(carry, block_id):
        cosine_part, sine_part = x_phase(block_id)
        inner_bwd = x_inverse(input_f, cosine_part, sine_part).astype(jnp.bfloat16)
        slope_grad = lax.dynamic_index_in_dim(slope_blocks, block_id, 0, keepdims=False).astype(jnp.float32)
        spectral_part = forward_scale * jnp.dot(inner_bwd, yinverse, preferred_element_type=jnp.float32)
        local_part = jnp.einsum('poxy,co->pcxy', slope_grad, local_f, precision=EXACT)
        return (carry, (spectral_part + local_part).astype(jnp.bfloat16))
    _, out_blocks = lax.scan(pass_three, jnp.zeros((), jnp.float32), block_ids)
    grad_field = jnp.transpose(out_blocks, (1, 2, 0, 3, 4)).reshape(PLANES, C, NX, NY)
    return (grad_field, grad_spectral, grad_local)
```

```python
import math

import jax
import jax.numpy as jnp
import numpy as np
from jax import lax
from jax.sharding import PartitionSpec as P

NX = 2048
NY = 2048
C = 64
MX = 64
MY = 64
TWO_PI = 2.0 * math.pi
ROOT_HALF = 1.0 / math.sqrt(2.0)
ROOT_TWO_PI = 1.0 / math.sqrt(2.0 * math.pi)
BF = jnp.bfloat16
F32 = jnp.float32


def tables(grid_shards, cells_x, cells_y):
    coords = np.arange(cells_y)[:, None] * np.arange(MY)[None, :] % NY
    angle = coords * (TWO_PI / NY)
    pair = np.stack([np.cos(angle), -np.sin(angle)], axis=1).reshape(cells_y, 2, 2, 32)
    ytable = np.transpose(pair, (0, 2, 1, 3)).reshape(cells_y, 128)
    mode_ids = np.arange(MX)
    frequency = np.where(mode_ids < MX // 2, mode_ids, mode_ids + NX - MX)
    cells = np.arange(grid_shards * cells_x)
    xangle = (frequency[:, None] * cells[None, :] % NX) * (TWO_PI / NX)
    xphase = np.stack([np.cos(xangle), np.sin(xangle)]).reshape(2, MX, grid_shards, cells_x)
    return ytable.astype(np.float32), np.transpose(xphase, (2, 0, 1, 3)).astype(np.float32)


def gelu_slope(values):
    return (
        0.5 * (1.0 + jax.scipy.special.erf(values * ROOT_HALF))
        + values * jnp.exp(-0.5 * values * values) * ROOT_TWO_PI
    )


def turn(values, sign):
    parts = values.reshape(values.shape[:-1] + (2, 2, 32))
    return jnp.stack([sign * parts[..., 1, :], -sign * parts[..., 0, :]], axis=-2).reshape(values.shape)


def swap_cores(values):
    return lax.ppermute(values, "gy", [(0, 1), (1, 0)])


def on_device(field, cotangent, local_weight, spectral_weight):
    field = field[0]
    cotangent = cotangent[0]
    weights = spectral_weight[0]
    channels, cells_x, cells_y = field.shape
    shards = lax.axis_size("gx")
    core = lax.axis_index("gy")
    ytable, xphase = tables(shards, cells_x, cells_y)
    ytable = jnp.asarray(ytable, BF)
    phase = lax.dynamic_index_in_dim(jnp.asarray(xphase, BF), lax.axis_index("gx"), 0, keepdims=False)
    lane = jnp.arange(128, dtype=jnp.int32)
    parity = jnp.where(lane % 2 * core == 1, -1.0, 1.0).astype(F32)

    def partial_modes(values, scale):
        parts = jnp.dot(values.reshape(-1, cells_y), ytable, preferred_element_type=F32)
        parts = parts.reshape(2, 32, cells_x, 2, 64)
        parts = jnp.where(core == 0, parts, parts[:, :, :, ::-1])
        parts = jnp.transpose(parts, (3, 1, 2, 0, 4)).reshape(2, 32, cells_x, 128) * parity
        total = parts[0] + swap_cores(parts[1].astype(BF)).astype(F32)
        pair = jnp.stack([total, turn(total, 1.0)]).astype(BF)
        modes = jnp.einsum("qmx,qrxl->mrl", phase, pair, preferred_element_type=F32)
        return (modes * scale).astype(BF)

    def exchange(rows):
        return lax.all_to_all(rows, "gx", 0, 0, tiled=True)

    def spread(modes):
        pair = jnp.stack([modes, turn(modes, -1.0)])
        inner = jnp.einsum("qmx,qmrl->rxl", phase, pair, preferred_element_type=F32)
        inner = inner.astype(BF)
        other = swap_cores(inner)
        halves = jnp.stack([jnp.where(core == 0, inner, other), jnp.where(core == 0, other, inner)])
        halves = halves * parity.astype(BF)
        halves = halves.reshape(2, 32, cells_x, 2, 64)
        return jnp.transpose(halves, (3, 1, 2, 0, 4)).reshape(channels * cells_x, 128)

    def to_rows(spec):
        return jnp.transpose(spec.reshape(32, 2, 2, 32), (3, 2, 1, 0)).reshape(32, 128)

    def from_rows(rows):
        return jnp.transpose(rows.reshape(32, 2, 2, 32), (3, 2, 1, 0)).reshape(32, 2, 64)

    sent = exchange(partial_modes(field, 1.0 / math.sqrt(NX * NY)))
    spectrum = from_rows(jnp.sum(sent.astype(F32), axis=0)).astype(BF)
    real_in, imag_in = spectrum[:, 0], spectrum[:, 1]
    from_real = jnp.einsum("kc,kco->ko", real_in, weights, preferred_element_type=F32)
    from_imag = jnp.einsum("kc,kco->ko", imag_in, weights, preferred_element_type=F32)
    mixed = jnp.stack(
        [from_real[..., :C] - from_imag[..., C:], from_real[..., C:] + from_imag[..., :C]], axis=1
    ).astype(BF)
    inner_fwd = spread(exchange(jnp.broadcast_to(to_rows(mixed)[None], (shards, 32, 128))))
    spatial = (1.0 / math.sqrt(MX * MY)) * jnp.dot(inner_fwd, ytable.T, preferred_element_type=F32)
    pre_act = spatial.reshape(channels, cells_x, cells_y) + jnp.einsum(
        "cxy,co->oxy", field, local_weight, preferred_element_type=F32
    )
    slope_grad = (cotangent.astype(F32) * gelu_slope(pre_act)).astype(BF)
    weight_part = jnp.einsum("cxy,oxy->co", field, slope_grad, preferred_element_type=F32)
    high = weight_part.astype(BF)
    low = (weight_part - high.astype(F32)).astype(BF)
    rider = jnp.concatenate([high, low], axis=1)[:, None, :]
    rider = jnp.concatenate([rider, jnp.zeros((C, 7, 128), BF)], axis=1)
    part = partial_modes(slope_grad, 1.0 / math.sqrt(MX * MY))
    sent = jnp.sum(exchange(jnp.concatenate([part, rider], axis=1)).astype(F32), axis=0)
    mode_grad = from_rows(sent[:32]).astype(BF)
    row = sent[32, :C] + sent[32, C:]
    row_high = row.astype(BF)
    row_low = (row - row_high.astype(F32)).astype(BF)
    row = jnp.concatenate([row_high, row_low])[None]
    grad_real, grad_imag = mode_grad[:, 0], mode_grad[:, 1]
    left_pair = jnp.concatenate([grad_real, grad_imag], axis=-1)
    right_pair = jnp.concatenate([grad_imag, -grad_real], axis=-1)
    gamma = math.sqrt(MX * MY / (NX * NY))
    grad_spectral = gamma * (
        real_in.astype(F32)[:, :, None] * left_pair.astype(F32)[:, None, :]
        + imag_in.astype(F32)[:, :, None] * right_pair.astype(F32)[:, None, :]
    )
    input_modes = jnp.stack(
        [
            jnp.einsum("ko,kco->kc", left_pair, weights, preferred_element_type=F32),
            jnp.einsum("ko,kco->kc", right_pair, weights, preferred_element_type=F32),
        ],
        axis=1,
    ).astype(BF)
    rows = jnp.concatenate([to_rows(input_modes), row, jnp.zeros((7, 128), BF)], axis=0)
    got = exchange(jnp.broadcast_to(rows[None], (shards, 40, 128)))
    core_part = got[:, 32, :C].astype(F32) + got[:, 32, C:].astype(F32)
    grad_local = (core_part + swap_cores(core_part)) * (1.0 / math.sqrt(NX * NY))
    inner_bwd = spread(got[:, :32])
    spectral_part = (1.0 / math.sqrt(NX * NY)) * jnp.dot(inner_bwd, ytable.T, preferred_element_type=F32)
    local_part = jnp.einsum("oxy,co->cxy", slope_grad, local_weight, preferred_element_type=F32)
    grad_field = (spectral_part.reshape(channels, cells_x, cells_y) + local_part).astype(BF)
    return (grad_field[None], grad_spectral[None], grad_local)


def solution(mesh):
    placed = (P(None, None, "gx", "gy"), P(None, None, "gx", "gy"), P(), P("gx", "gy", None, None))
    return jax.shard_map(
        on_device,
        mesh=mesh,
        in_specs=placed,
        out_specs=(P(None, None, "gx", "gy"), P("gx", "gy", None, None), P()),
        check_vma=False,
    )
```

```python
import math

import jax
import jax.experimental.pallas as pl
import jax.experimental.pallas.tpu as pltpu
import jax.numpy as jnp
import numpy as np
from jax import lax
from jax.sharding import PartitionSpec as P

NX = 2048
NY = 2048
C = 64
MX = 64
MY = 64
SHARDS = 64
XC = 32
YC = 1024
YB = 256
TWO_PI = 2.0 * math.pi
ROOT_HALF = 1.0 / math.sqrt(2.0)
ROOT_TWO_PI = 1.0 / math.sqrt(2.0 * math.pi)
FORWARD = 1.0 / math.sqrt(NX * NY)
INVERSE = 1.0 / math.sqrt(MX * MY)
GAMMA = math.sqrt(MX * MY / (NX * NY))
BF = jnp.bfloat16
F32 = jnp.float32
RIDER = 8


def tables():
    angle = (np.arange(YC)[:, None] * np.arange(MY)[None, :] % NY) * (TWO_PI / NY)
    pair = np.stack([np.cos(angle), -np.sin(angle)], axis=1).reshape(YC, 2, 2, 32)
    forth = np.transpose(pair, (0, 2, 1, 3)).reshape(YC, 128)
    back = forth.T.reshape(2, 1, 64, YC)
    back = np.concatenate([back, back], axis=1).reshape(256, YC)
    modes = np.arange(MX)
    frequency = np.where(modes < MX // 2, modes, modes + NX - MX)
    xangle = (frequency[:, None] * np.arange(NX)[None, :] % NX) * (TWO_PI / NX)
    phase = np.stack([np.cos(xangle), np.sin(xangle)]).reshape(2, MX, SHARDS, XC)
    return forth, back, np.transpose(phase, (2, 0, 1, 3)), np.transpose(phase, (2, 0, 3, 1))


def dot(a, b, dims=((1,), (0,))):
    return lax.dot_general(a, b, (dims, ((), ())), preferred_element_type=F32)


def iota(shape, axis):
    return lax.broadcasted_iota(jnp.int32, shape, axis)


def turn(values, sign):
    lane = iota(values.shape, 1)
    first = lane % 64 < 32
    return jnp.where(first, sign * pltpu.roll(values, 96, 1), -sign * pltpu.roll(values, 32, 1))


def parity(core, shape):
    return jnp.where((iota(shape, len(shape) - 1) % 2) * core == 1, -1.0, 1.0).astype(F32)


def split_halves(parts, cells, groups, core, own_ref, other_ref):
    rows = cells * groups * 8
    blocks = parts.reshape(cells * groups, 2, 8, 128)
    first = blocks[:, 0].reshape(rows, 128)
    second = blocks[:, 1].reshape(rows, 128)
    low = iota((rows, 128), 1) < 64
    sign = parity(core, (rows, 128))
    half_a = jnp.where(low, first, pltpu.roll(second, 64, 1)) * sign
    half_b = jnp.where(low, pltpu.roll(first, 64, 1), second) * sign
    own = jnp.where(core == 0, half_a, half_b)
    other = jnp.where(core == 0, half_b, half_a)
    own_ref[...] = own.reshape(cells, groups * 8, 128).astype(BF)
    other_ref[...] = other.reshape(cells, groups * 8, 128).astype(BF)


def y_forward_kernel(place, field_ref, forth_ref, cells_ref, own_ref, other_ref):
    rows = jnp.swapaxes(field_ref[...], 0, 1)
    cells_ref[...] = rows
    parts = dot(rows.reshape(16 * 32, YC), forth_ref[...])
    split_halves(parts, 16, 2, place[1], own_ref, other_ref)


def y_forward(place, field, forth):
    part = pl.BlockSpec((16, 16, 128), lambda g, h, s: (h, g, 0))
    return pl.pallas_call(
        y_forward_kernel,
        grid_spec=pltpu.PrefetchScalarGridSpec(
            num_scalar_prefetch=1,
            grid=(2, 2),
            in_specs=[
                pl.BlockSpec((32, 16, YC), lambda g, h, s: (g, h, 0)),
                pl.BlockSpec((YC, 128), lambda g, h, s: (0, 0)),
            ],
            out_specs=[pl.BlockSpec((16, 32, YC), lambda g, h, s: (h, g, 0)), part, part],
        ),
        out_shape=[
            jax.ShapeDtypeStruct((XC, C, YC), BF),
            jax.ShapeDtypeStruct((XC, 32, 128), BF),
            jax.ShapeDtypeStruct((XC, 32, 128), BF),
        ],
        compiler_params=pltpu.CompilerParams(vmem_limit_bytes=20 << 20),
        name="y_forward",
    )(place, field, forth)


def x_forward_kernel(scale, place, phase_ref, own_ref, other_ref, *rest):
    out_ref = rest[-1]
    total = own_ref[...].astype(F32) + other_ref[...].astype(F32)
    widen = (iota((XC, 256), 1) // 8 == iota((XC, 256), 0)).astype(BF)
    keep = iota((1, 8, 256), 2) % 8 == iota((1, 8, 256), 1)
    left = []
    for q in range(2):
        wide = dot(phase_ref[0, q], widen)
        left.append(jnp.where(keep, wide[:, None, :], 0.0).reshape(512, 256).astype(BF))
    left = jnp.concatenate(left, axis=1)
    for g in range(2):
        right = []
        for s in range(2):
            rows = total[:, 16 * g + 8 * s : 16 * g + 8 * s + 8].reshape(256, 128)
            right.append(jnp.concatenate([rows, turn(rows, 1.0)], axis=0))
        modes = dot(left, jnp.concatenate(right, axis=1).astype(BF)) * scale
        both = [modes[:, 128 * s : 128 * s + 128].reshape(64, 8, 128) for s in range(2)]
        out_ref[:, 16 * g : 16 * g + 16, :] = jnp.concatenate(both, axis=1).astype(BF)
    if len(rest) == 2:
        rider = rest[0][...].astype(F32)
        out_ref[:, 32:, :] = jnp.broadcast_to(rider[:, None, :], (64, RIDER, 128)).astype(BF)


def x_forward(place, phase, own, other, scale, rider=None):
    rows = 32 if rider is None else 32 + RIDER
    operands = [own, other] + ([] if rider is None else [rider])

    def whole(a):
        return pl.BlockSpec(a.shape, lambda i, s: (0,) * a.ndim)

    return pl.pallas_call(
        lambda *refs: x_forward_kernel(scale, *refs),
        grid_spec=pltpu.PrefetchScalarGridSpec(
            num_scalar_prefetch=1,
            grid=(1,),
            in_specs=[pl.BlockSpec((1, 2, MX, XC), lambda i, s: (s[0], 0, 0, 0))]
            + [whole(a) for a in operands],
            out_specs=pl.BlockSpec((SHARDS, rows, 128), lambda i, s: (0, 0, 0)),
        ),
        out_shape=jax.ShapeDtypeStruct((SHARDS, rows, 128), BF),
        compiler_params=pltpu.CompilerParams(vmem_limit_bytes=20 << 20),
        name="x_forward",
    )(place, phase, *operands)


def x_inverse_kernel(place, phase_ref, sent_ref, inner_ref):
    widen = (iota((MX, 512), 1) // 8 == iota((MX, 512), 0)).astype(BF)
    keep = iota((1, 8, 512), 2) % 8 == iota((1, 8, 512), 1)
    left = []
    for q in range(2):
        wide = dot(phase_ref[0, q], widen)
        left.append(jnp.where(keep, wide[:, None, :], 0.0).reshape(256, 512).astype(BF))
    left = jnp.concatenate(left, axis=0)
    for g in range(2):
        rows = sent_ref[:, 16 * g : 16 * g + 16, :].astype(F32)
        right = [rows[:, 8 * s : 8 * s + 8].reshape(512, 128) for s in range(2)]
        both = dot(left, jnp.concatenate(right, axis=1).astype(BF))
        inner = []
        for s in range(2):
            piece = both[:, 128 * s : 128 * s + 128]
            inner.append((piece[:256] + turn(piece[256:], -1.0)).reshape(XC, 8, 128))
        inner_ref[:XC, 16 * g : 16 * g + 16, :] = jnp.concatenate(inner, axis=1).astype(BF)
    if sent_ref.shape[1] > 32:
        rider = sent_ref[:, 32:, :].astype(F32)[:, 0, :]
        inner_ref[XC:, :, :] = rider.reshape(2, 32, 128).astype(BF)


def x_inverse(place, phase, sent):
    cells = XC if sent.shape[1] == 32 else XC + 2
    return pl.pallas_call(
        x_inverse_kernel,
        grid_spec=pltpu.PrefetchScalarGridSpec(
            num_scalar_prefetch=1,
            grid=(1,),
            in_specs=[
                pl.BlockSpec((1, 2, XC, MX), lambda i, s: (s[0], 0, 0, 0)),
                pl.BlockSpec(sent.shape, lambda i, s: (0, 0, 0)),
            ],
            out_specs=pl.BlockSpec((cells, 32, 128), lambda i, s: (0, 0, 0)),
        ),
        out_shape=jax.ShapeDtypeStruct((cells, 32, 128), BF),
        compiler_params=pltpu.CompilerParams(vmem_limit_bytes=20 << 20),
        name="x_inverse",
    )(place, phase, sent)


def pick(b):
    r = iota((32, C), 0)
    return (iota((32, C), 1) == (r // 8) * 16 + b * 8 + r % 8).astype(BF)


def modes_of(rows):
    flipped = rows.T.astype(BF)
    return (dot(flipped[:64], pick(0)) + dot(flipped[64:], pick(1))).astype(BF)


def rows_of(real, imag):
    blocks = [dot(pick(b), part, ((1,), (1,))) for b in range(2) for part in (real, imag)]
    return jnp.concatenate(blocks, axis=1)


def own_mode(shape):
    return iota(shape, 1) // C == iota(shape, 0) % 32


def mix_kernel(sent_ref, weight_ref, out_ref, spectrum_ref):
    spectrum = modes_of(jnp.sum(sent_ref[...].astype(F32), axis=0))
    spectrum_ref[...] = spectrum
    pair = spectrum.astype(F32)
    pair = jnp.concatenate([pair, pair], axis=1)
    wide = jnp.concatenate([pair] * 16, axis=1)
    wide = jnp.where(own_mode(wide.shape), wide, 0.0).astype(BF)
    product = dot(wide, weight_ref[...].reshape(32 * C, 128))
    lane = iota((32, 128), 1)
    mixed = product[:32] + jnp.where(lane < 64, -1.0, 1.0) * pltpu.roll(product[32:], 64, 1)
    mixed = mixed.astype(BF)
    rows = rows_of(mixed[:, :64], mixed[:, 64:])
    out_ref[...] = jnp.broadcast_to(rows[None], (SHARDS, 32, 128)).astype(BF)


def mix(sent, weights):
    return pl.pallas_call(
        mix_kernel,
        out_shape=[
            jax.ShapeDtypeStruct((SHARDS, 32, 128), BF),
            jax.ShapeDtypeStruct((64, C), BF),
        ],
        compiler_params=pltpu.CompilerParams(vmem_limit_bytes=20 << 20),
        name="mix",
    )(sent, weights)


def mix_back_kernel(sent_ref, weight_ref, out_ref, pair_ref):
    total = jnp.sum(sent_ref[...].astype(F32), axis=0)
    modes = modes_of(total[:32]).astype(F32)
    real, imag = modes[:32], modes[32:]
    left = jnp.concatenate([real, imag], axis=1)
    right = jnp.concatenate([imag, -real], axis=1)
    pair = jnp.concatenate([left, right], axis=0).astype(BF)
    pair_ref[...] = pair
    product = dot(pair, weight_ref[...].reshape(32 * C, 128), ((1,), (1,)))
    product = jnp.where(own_mode(product.shape), product, 0.0)
    folded = product[:, :128]
    for k in range(1, 16):
        folded = folded + product[:, 128 * k : 128 * k + 128]
    folded = (folded + pltpu.roll(folded, 64, 1))[:, :64].astype(BF)
    rows = rows_of(folded[:32], folded[32:])
    rider = total[32:]
    rider = rider + pltpu.roll(rider, 64, 1)
    high = rider.astype(BF).astype(F32)
    rider = jnp.where(iota(rider.shape, 1) < 64, high, rider - high)
    rows = jnp.concatenate([rows, rider], axis=0)
    out_ref[...] = jnp.broadcast_to(rows[None], (SHARDS, 32 + RIDER, 128)).astype(BF)


def mix_back(sent, weights):
    return pl.pallas_call(
        mix_back_kernel,
        out_shape=[
            jax.ShapeDtypeStruct((SHARDS, 32 + RIDER, 128), BF),
            jax.ShapeDtypeStruct((64, 128), BF),
        ],
        compiler_params=pltpu.CompilerParams(vmem_limit_bytes=20 << 20),
        name="mix_back",
    )(sent, weights)


def outer_kernel(spectrum_ref, pair_ref, out_ref):
    flipped = spectrum_ref[...].astype(F32).T
    tall = jnp.concatenate([flipped] * 8, axis=0)
    shape = tall.shape
    keep = iota(shape, 1) % 32 == iota(shape, 0) // C + 8 * pl.program_id(0)
    tall = jnp.where(keep, tall, 0.0).astype(BF)
    out_ref[...] = (dot(tall, pair_ref[...]) * GAMMA).reshape(8, C, 128)


def outer(spectrum, pair):
    return pl.pallas_call(
        outer_kernel,
        grid=(4,),
        in_specs=[pl.BlockSpec((64, C), lambda i: (0, 0)), pl.BlockSpec((64, 128), lambda i: (0, 0))],
        out_specs=pl.BlockSpec((8, C, 128), lambda i: (i, 0, 0)),
        out_shape=jax.ShapeDtypeStruct((32, C, 128), F32),
        compiler_params=pltpu.CompilerParams(vmem_limit_bytes=20 << 20),
        cost_estimate=pl.CostEstimate(flops=2 * 2048 * 64 * 128, bytes_accessed=1 << 20, transcendentals=0),
        name="outer",
    )(spectrum, pair)


def gelu_slope(values):
    return (
        0.5 * (1.0 + lax.erf(values * ROOT_HALF))
        + values * jnp.exp(-0.5 * values * values) * ROOT_TWO_PI
    )


def block_diagonal(square):
    wide = jnp.concatenate([square, square], axis=1)
    wide = jnp.concatenate([wide, wide], axis=1)
    full = jnp.concatenate([wide] * 4, axis=0)
    return jnp.where(iota(full.shape, 0) // C == iota(full.shape, 1) // C, full, 0.0)


def inner_rows(core, scale, own_ref, other_ref, rows_ref):
    own = own_ref[...].astype(F32)
    other = other_ref[...].astype(F32)
    shape = own.shape
    sign = parity(core, shape) * scale
    for half in range(2):
        values = jnp.where(core == half, own, other) * sign
        values = values.reshape(shape[0] * 4, 8, 128)
        low = iota(values.shape, 2) < 64
        first = jnp.where(low, values, 0.0)
        second = values - first
        both = jnp.stack([first, second], axis=1).reshape(shape[0] * C, 128)
        rows_ref[:, 128 * half : 128 * half + 128] = both.astype(BF)


def cells_kernel(
    place,
    field_ref,
    cotangent_ref,
    own_in_ref,
    other_in_ref,
    local_ref,
    forth_ref,
    back_ref,
    slope_ref,
    own_ref,
    other_ref,
    weight_ref,
    diagonal,
    inner,
    parts,
    products,
):
    half, block = pl.program_id(0), pl.program_id(1)

    @pl.when(jnp.logical_and(half == 0, block == 0))
    def _():
        diagonal[...] = block_diagonal(local_ref[...].astype(F32)).T.astype(BF)
        products[...] = jnp.zeros_like(products)

    @pl.when(block == 0)
    def _():
        inner_rows(place[1], INVERSE, own_in_ref, other_in_ref, inner)
        parts[...] = jnp.zeros_like(parts)

    cotangent = jnp.swapaxes(cotangent_ref[...], 0, 1)
    for g in range(4):
        rows = slice(256 * g, 256 * g + 256)
        field = field_ref[4 * g : 4 * g + 4].reshape(256, YB)
        pre_act = dot(diagonal[...], field) + dot(inner[rows, :], back_ref[...])
        upper = cotangent[4 * g : 4 * g + 4].reshape(256, YB).astype(F32)
        slope = (upper * gelu_slope(pre_act)).astype(BF)
        slope_ref[4 * g : 4 * g + 4] = slope.reshape(4, C, YB)
        products[...] += dot(field, slope, ((1,), (1,)))
        parts[rows, :] += dot(slope, forth_ref[...])

    @pl.when(block == YC // YB - 1)
    def _():
        split_halves(parts[...], 16, 4, place[1], own_ref, other_ref)

    @pl.when(jnp.logical_and(half == 1, block == YC // YB - 1))
    def _():
        total = products[...]
        first = total[:64, :128] + pltpu.roll(total[64:128, :128], 64, 1)
        first = first + total[128:192, 128:] + pltpu.roll(total[192:, 128:], 64, 1)
        high = first.astype(BF).astype(F32)
        low = pltpu.roll(first - high, 64, 1)
        weight_ref[...] = jnp.where(iota((64, 128), 1) < 64, high, low).astype(BF)


def cells_step(place, cells, cotangent, own, other, local_weight, forth, back):
    part = pl.BlockSpec((16, 32, 128), lambda h, i, s: (h, 0, 0))
    return pl.pallas_call(
        cells_kernel,
        grid_spec=pltpu.PrefetchScalarGridSpec(
            num_scalar_prefetch=1,
            grid=(2, YC // YB),
            in_specs=[
                pl.BlockSpec((16, C, YB), lambda h, i, s: (h, 0, i)),
                pl.BlockSpec((C, 16, YB), lambda h, i, s: (0, h, i)),
                part,
                part,
                pl.BlockSpec((C, C), lambda h, i, s: (0, 0)),
                pl.BlockSpec((YB, 128), lambda h, i, s: (i, 0)),
                pl.BlockSpec((256, YB), lambda h, i, s: (0, i)),
            ],
            out_specs=[
                pl.BlockSpec((16, C, YB), lambda h, i, s: (h, 0, i)),
                part,
                part,
                pl.BlockSpec((64, 128), lambda h, i, s: (0, 0)),
            ],
            scratch_shapes=[
                pltpu.VMEM((256, 256), BF),
                pltpu.VMEM((1024, 256), BF),
                pltpu.VMEM((1024, 128), F32),
                pltpu.VMEM((256, 256), F32),
            ],
        ),
        out_shape=[
            jax.ShapeDtypeStruct((XC, C, YC), BF),
            jax.ShapeDtypeStruct((XC, 32, 128), BF),
            jax.ShapeDtypeStruct((XC, 32, 128), BF),
            jax.ShapeDtypeStruct((64, 128), BF),
        ],
        compiler_params=pltpu.CompilerParams(vmem_limit_bytes=24 << 20),
        name="cells_step",
    )(place, cells, cotangent, own, other, local_weight, forth, back)


def last_kernel(
    place,
    slope_ref,
    own_in_ref,
    other_in_ref,
    own_tail_ref,
    other_tail_ref,
    local_ref,
    back_ref,
    out_ref,
    grad_local_ref,
    diagonal,
    inner,
):
    half, block = pl.program_id(0), pl.program_id(1)

    @pl.when(jnp.logical_and(half == 0, block == 0))
    def _():
        diagonal[...] = block_diagonal(local_ref[...].astype(F32)).astype(BF)
        total = own_tail_ref[...].astype(F32).reshape(64, 128)
        total = total + pltpu.roll(total, 64, 1)
        more = other_tail_ref[...].astype(F32).reshape(64, 128)
        more = more + pltpu.roll(more, 64, 1)
        grad_local_ref[...] = (total + more)[:, :64] * FORWARD

    @pl.when(block == 0)
    def _():
        inner_rows(place[1], FORWARD, own_in_ref, other_in_ref, inner)

    pieces = []
    for g in range(4):
        rows = slice(256 * g, 256 * g + 256)
        slope = slope_ref[4 * g : 4 * g + 4].reshape(256, YB)
        total = dot(diagonal[...], slope) + dot(inner[rows, :], back_ref[...])
        pieces.append(total.astype(BF).reshape(4, C, YB))
    out_ref[...] = jnp.swapaxes(jnp.concatenate(pieces, axis=0), 0, 1)


def last_step(place, slope, own, other, local_weight, back):
    part = pl.BlockSpec((16, 32, 128), lambda h, i, s: (h, 0, 0))
    tail = pl.BlockSpec((2, 32, 128), lambda h, i, s: (XC // 2, 0, 0))
    return pl.pallas_call(
        last_kernel,
        grid_spec=pltpu.PrefetchScalarGridSpec(
            num_scalar_prefetch=1,
            grid=(2, YC // YB),
            in_specs=[
                pl.BlockSpec((16, C, YB), lambda h, i, s: (h, 0, i)),
                part,
                part,
                tail,
                tail,
                pl.BlockSpec((C, C), lambda h, i, s: (0, 0)),
                pl.BlockSpec((256, YB), lambda h, i, s: (0, i)),
            ],
            out_specs=[
                pl.BlockSpec((C, 16, YB), lambda h, i, s: (0, h, i)),
                pl.BlockSpec((C, C), lambda h, i, s: (0, 0)),
            ],
            scratch_shapes=[pltpu.VMEM((256, 256), BF), pltpu.VMEM((1024, 256), BF)],
        ),
        out_shape=[
            jax.ShapeDtypeStruct((C, XC, YC), BF),
            jax.ShapeDtypeStruct((C, C), F32),
        ],
        compiler_params=pltpu.CompilerParams(vmem_limit_bytes=24 << 20),
        name="last_step",
    )(place, slope, own, other, own, other, local_weight, back)


def swap_cores(values):
    return lax.ppermute(values, "gy", [(0, 1), (1, 0)])


def exchange(rows):
    return lax.all_to_all(rows, "gx", 0, 0, tiled=True)


def on_device(field, cotangent, local_weight, spectral_weight):
    forth, back, phase, phase_back = [jnp.asarray(t.astype(np.float32), BF) for t in tables()]
    place = jnp.stack([lax.axis_index("gx"), lax.axis_index("gy")]).astype(jnp.int32)
    weights = spectral_weight[0]

    cells, own, other = y_forward(place, field[0], forth)
    sent = exchange(x_forward(place, phase, own, swap_cores(other), FORWARD))
    copies, spectrum = mix(sent, weights)
    inner = x_inverse(place, phase_back, exchange(copies))
    slope, own, other, rider = cells_step(
        place, cells, cotangent[0], inner, swap_cores(inner), local_weight, forth, back
    )
    sent = exchange(x_forward(place, phase, own, swap_cores(other), INVERSE, rider))
    copies, pair = mix_back(sent, weights)
    inner = x_inverse(place, phase_back, exchange(copies))
    grad_spectral = outer(spectrum, pair)
    grad_field, grad_local = last_step(place, slope, inner, swap_cores(inner), local_weight, back)
    return (grad_field[None], grad_spectral[None], grad_local)


def solution(mesh):
    placed = (P(None, None, "gx", "gy"), P(None, None, "gx", "gy"), P(), P("gx", "gy", None, None))
    return jax.shard_map(
        on_device,
        mesh=mesh,
        in_specs=placed,
        out_specs=(P(None, None, "gx", "gy"), P("gx", "gy", None, None), P()),
        check_vma=False,
    )
```

```python
import math

import jax
import jax.experimental.pallas as pl
import jax.experimental.pallas.tpu as pltpu
import jax.numpy as jnp
import numpy as np
from jax import lax
from jax.sharding import PartitionSpec as P

NX = 2048
NY = 2048
C = 64
MX = 64
MY = 64
SHARDS = 64
XC = 32
YC = 1024
YB = 256
YO = 512
TWO_PI = 2.0 * math.pi
ROOT_HALF = 1.0 / math.sqrt(2.0)
ROOT_TWO_PI = 1.0 / math.sqrt(2.0 * math.pi)
FORWARD = 1.0 / math.sqrt(NX * NY)
INVERSE = 1.0 / math.sqrt(MX * MY)
GAMMA = math.sqrt(MX * MY / (NX * NY))
BF = jnp.bfloat16
F32 = jnp.float32
RIDER = 8


def tables():
    angle = (np.arange(YC)[:, None] * np.arange(MY)[None, :] % NY) * (TWO_PI / NY)
    pair = np.stack([np.cos(angle), -np.sin(angle)], axis=1).reshape(YC, 2, 2, 32)
    forth = np.transpose(pair, (0, 2, 1, 3)).reshape(YC, 128)
    modes = np.arange(MX)
    frequency = np.where(modes < MX // 2, modes, modes + NX - MX)
    xangle = (frequency[:, None] * np.arange(XC)[None, :] % NX) * (TWO_PI / NX)
    phase = np.stack([np.cos(xangle), np.sin(xangle)])
    origin = (modes[:, None] * np.arange(SHARDS)[None, :] % SHARDS) * (TWO_PI / SHARDS)
    return forth, forth.T, phase, np.stack([np.cos(origin), np.sin(origin)])


def dot(a, b, dims=((1,), (0,))):
    return lax.dot_general(a, b, (dims, ((), ())), preferred_element_type=F32)


VMEM = pl.BlockSpec(memory_space=pltpu.VMEM)
SMEM = pl.BlockSpec(memory_space=pltpu.SMEM)


def iota(shape, axis):
    return lax.broadcasted_iota(jnp.int32, shape, axis)


def turn(values, sign):
    lane = iota(values.shape, 1)
    first = lane % 64 < 32
    return jnp.where(first, sign * pltpu.roll(values, 96, 1), -sign * pltpu.roll(values, 32, 1))


def parity(core, shape):
    return jnp.where((iota(shape, len(shape) - 1) % 2) * core == 1, -1.0, 1.0).astype(F32)


def split_halves(parts, cells, groups, core):
    rows = cells * groups * 8
    blocks = parts.reshape(cells * groups, 2, 8, 128)
    first = blocks[:, 0].reshape(rows, 128)
    second = blocks[:, 1].reshape(rows, 128)
    low = iota((rows, 128), 1) < 64
    sign = parity(core, (rows, 128))
    half_a = jnp.where(low, first, pltpu.roll(second, 64, 1)) * sign
    half_b = jnp.where(low, pltpu.roll(first, 64, 1), second) * sign
    own = jnp.where(core == 0, half_a, half_b)
    other = jnp.where(core == 0, half_b, half_a)
    shape = (cells, groups * 8, 128)
    return own.reshape(shape).astype(BF), other.reshape(shape).astype(BF)


def y_forward_kernel(place, field_ref, forth_ref, cells_ref, own_ref, other_ref, held, arrived):
    def copy(k):
        group, half = k // 2, k % 2
        channels = pl.ds(pl.multiple_of(32 * group, 32), 32)
        cells = pl.ds(pl.multiple_of(16 * half, 16), 16)
        return pltpu.make_async_copy(field_ref.at[channels, cells], held.at[k], arrived.at[k])

    for k in range(4):
        copy(k).start()

    @pl.loop(0, 4)
    def _(k):
        group, half = k // 2, k % 2
        copy(k).wait()
        rows = jnp.swapaxes(held[k], 0, 1)
        cells = pl.ds(pl.multiple_of(16 * half, 16), 16)
        cells_ref[cells, pl.ds(pl.multiple_of(32 * group, 32), 32), :] = rows
        parts = dot(rows.reshape(16 * 32, YC), forth_ref[...])
        own, other = split_halves(parts, 16, 2, place[1])
        channels = pl.ds(pl.multiple_of(16 * group, 16), 16)
        own_ref[cells, channels, :] = own
        other_ref[cells, channels, :] = other


def y_forward(place, field, forth):
    return pl.pallas_call(
        y_forward_kernel,
        in_specs=[SMEM, pl.BlockSpec(memory_space=pltpu.HBM), VMEM],
        out_specs=[VMEM, VMEM, VMEM],
        out_shape=[
            pltpu.VMEM((XC, C, YC), BF),
            pltpu.VMEM((XC, 32, 128), BF),
            pltpu.VMEM((XC, 32, 128), BF),
        ],
        scratch_shapes=[pltpu.VMEM((4, 32, 16, YC), BF), pltpu.SemaphoreType.DMA((4,))],
        compiler_params=pltpu.CompilerParams(vmem_limit_bytes=16 << 20),
        name="y_forward",
    )(place, pltpu.with_memory_space_constraint(field, pltpu.HBM), forth)


def rotated(phase_ref, origin_ref, shard, axis):
    at = iota((MX, SHARDS), 1 - axis) == shard
    cosine, sine = [
        jnp.sum(jnp.where(at, origin_ref[q], 0.0), axis=1 - axis, keepdims=True) for q in range(2)
    ]
    real, imag = phase_ref[0], phase_ref[1]
    return (cosine * real - sine * imag).astype(BF), (sine * real + cosine * imag).astype(BF)


def x_forward_kernel(scale, place, phase_ref, origin_ref, own_ref, other_ref, *rest):
    out_ref = rest[-1]
    total = own_ref[...].astype(F32) + other_ref[...].astype(F32)
    widen = (iota((XC, 256), 1) // 8 == iota((XC, 256), 0)).astype(BF)
    keep = iota((1, 8, 256), 2) % 8 == iota((1, 8, 256), 1)
    left = []
    for table in rotated(phase_ref, origin_ref, place[0], 0):
        wide = dot(table, widen)
        left.append(jnp.where(keep, wide[:, None, :], 0.0).reshape(512, 256).astype(BF))
    left = jnp.concatenate(left, axis=1)
    for g in range(2):
        right = []
        for s in range(2):
            rows = total[:, 16 * g + 8 * s : 16 * g + 8 * s + 8].reshape(256, 128)
            right.append(jnp.concatenate([rows, turn(rows, 1.0)], axis=0))
        modes = dot(left, jnp.concatenate(right, axis=1).astype(BF)) * scale
        both = [modes[:, 128 * s : 128 * s + 128].reshape(64, 8, 128) for s in range(2)]
        out_ref[:, 16 * g : 16 * g + 16, :] = jnp.concatenate(both, axis=1).astype(BF)
    if len(rest) == 2:
        rider = rest[0][...].astype(F32)
        out_ref[:, 32:, :] = jnp.broadcast_to(rider[:, None, :], (64, RIDER, 128)).astype(BF)


def x_forward(place, phase, origin, own, other, scale, rider=None):
    rows = 32 if rider is None else 32 + RIDER
    operands = [own, other] + ([] if rider is None else [rider])
    return pl.pallas_call(
        lambda *refs: x_forward_kernel(scale, *refs),
        in_specs=[SMEM, VMEM, VMEM] + [VMEM] * len(operands),
        out_specs=VMEM,
        out_shape=pltpu.VMEM((SHARDS, rows, 128), BF),
        compiler_params=pltpu.CompilerParams(vmem_limit_bytes=16 << 20),
        name="x_forward",
    )(place, phase, origin, *operands)


def x_inverse_kernel(place, phase_ref, origin_ref, sent_ref, inner_ref):
    widen = (iota((MX, 512), 1) // 8 == iota((MX, 512), 0)).astype(BF)
    keep = iota((1, 8, 512), 2) % 8 == iota((1, 8, 512), 1)
    left = []
    for table in rotated(phase_ref, origin_ref, place[0], 1):
        wide = dot(table, widen)
        left.append(jnp.where(keep, wide[:, None, :], 0.0).reshape(256, 512).astype(BF))
    left = jnp.concatenate(left, axis=0)
    for g in range(2):
        rows = sent_ref[:, 16 * g : 16 * g + 16, :].astype(F32)
        right = [rows[:, 8 * s : 8 * s + 8].reshape(512, 128) for s in range(2)]
        both = dot(left, jnp.concatenate(right, axis=1).astype(BF))
        inner = []
        for s in range(2):
            piece = both[:, 128 * s : 128 * s + 128]
            inner.append((piece[:256] + turn(piece[256:], -1.0)).reshape(XC, 8, 128))
        inner_ref[:XC, 16 * g : 16 * g + 16, :] = jnp.concatenate(inner, axis=1).astype(BF)
    if sent_ref.shape[1] > 32:
        rider = sent_ref[:, 32:, :].astype(F32)[:, 0, :]
        inner_ref[XC:, :, :] = rider.reshape(2, 32, 128).astype(BF)


def x_inverse(place, phase, origin, sent):
    cells = XC if sent.shape[1] == 32 else XC + 2
    return pl.pallas_call(
        x_inverse_kernel,
        in_specs=[SMEM, VMEM, VMEM, VMEM],
        out_specs=VMEM,
        out_shape=pltpu.VMEM((cells, 32, 128), BF),
        compiler_params=pltpu.CompilerParams(vmem_limit_bytes=16 << 20),
        name="x_inverse",
    )(place, phase, origin, sent)


def pick(b):
    r = iota((32, C), 0)
    return (iota((32, C), 1) == (r // 8) * 16 + b * 8 + r % 8).astype(BF)


def modes_of(rows):
    flipped = rows.T.astype(BF)
    return (dot(flipped[:64], pick(0)) + dot(flipped[64:], pick(1))).astype(BF)


def rows_of(real, imag):
    blocks = [dot(pick(b), part, ((1,), (1,))) for b in range(2) for part in (real, imag)]
    return jnp.concatenate(blocks, axis=1)


def own_mode(shape):
    return iota(shape, 1) // C == iota(shape, 0) % 32


def mix_kernel(sent_ref, weight_ref, out_ref, spectrum_ref):
    spectrum = modes_of(jnp.sum(sent_ref[...].astype(F32), axis=0))
    spectrum_ref[...] = spectrum
    pair = spectrum.astype(F32)
    pair = jnp.concatenate([pair, pair], axis=1)
    wide = jnp.concatenate([pair] * 16, axis=1)
    wide = jnp.where(own_mode(wide.shape), wide, 0.0).astype(BF)
    product = dot(wide, weight_ref[...].reshape(32 * C, 128))
    lane = iota((32, 128), 1)
    mixed = product[:32] + jnp.where(lane < 64, -1.0, 1.0) * pltpu.roll(product[32:], 64, 1)
    mixed = mixed.astype(BF)
    rows = rows_of(mixed[:, :64], mixed[:, 64:])
    out_ref[...] = jnp.broadcast_to(rows[None], (SHARDS, 32, 128)).astype(BF)


def mix(sent, weights):
    return pl.pallas_call(
        mix_kernel,
        out_shape=[
            jax.ShapeDtypeStruct((SHARDS, 32, 128), BF),
            jax.ShapeDtypeStruct((64, C), BF),
        ],
        compiler_params=pltpu.CompilerParams(vmem_limit_bytes=20 << 20),
        name="mix",
    )(sent, weights)


def mix_back_kernel(sent_ref, weight_ref, out_ref, pair_ref):
    total = jnp.sum(sent_ref[...].astype(F32), axis=0)
    modes = modes_of(total[:32]).astype(F32)
    real, imag = modes[:32], modes[32:]
    left = jnp.concatenate([real, imag], axis=1)
    right = jnp.concatenate([imag, -real], axis=1)
    pair = jnp.concatenate([left, right], axis=0).astype(BF)
    pair_ref[...] = pair
    product = dot(pair, weight_ref[...].reshape(32 * C, 128), ((1,), (1,)))
    product = jnp.where(own_mode(product.shape), product, 0.0)
    folded = product[:, :128]
    for k in range(1, 16):
        folded = folded + product[:, 128 * k : 128 * k + 128]
    folded = (folded + pltpu.roll(folded, 64, 1))[:, :64].astype(BF)
    rows = rows_of(folded[:32], folded[32:])
    rider = total[32:]
    rider = rider + pltpu.roll(rider, 64, 1)
    high = rider.astype(BF).astype(F32)
    rider = jnp.where(iota(rider.shape, 1) < 64, high, rider - high)
    rows = jnp.concatenate([rows, rider], axis=0)
    out_ref[...] = jnp.broadcast_to(rows[None], (SHARDS, 32 + RIDER, 128)).astype(BF)


def mix_back(sent, weights):
    return pl.pallas_call(
        mix_back_kernel,
        out_shape=[
            jax.ShapeDtypeStruct((SHARDS, 32 + RIDER, 128), BF),
            jax.ShapeDtypeStruct((64, 128), BF),
        ],
        compiler_params=pltpu.CompilerParams(vmem_limit_bytes=20 << 20),
        name="mix_back",
    )(sent, weights)


def outer_kernel(spectrum_ref, pair_ref, out_ref):
    flipped = spectrum_ref[...].astype(F32).T
    tall = jnp.concatenate([flipped] * 8, axis=0)
    shape = tall.shape
    keep = iota(shape, 1) % 32 == iota(shape, 0) // C + 8 * pl.program_id(0)
    tall = jnp.where(keep, tall, 0.0).astype(BF)
    out_ref[...] = (dot(tall, pair_ref[...]) * GAMMA).reshape(8, C, 128)


def outer(spectrum, pair):
    return pl.pallas_call(
        outer_kernel,
        grid=(4,),
        in_specs=[pl.BlockSpec((64, C), lambda i: (0, 0)), pl.BlockSpec((64, 128), lambda i: (0, 0))],
        out_specs=pl.BlockSpec((8, C, 128), lambda i: (i, 0, 0)),
        out_shape=jax.ShapeDtypeStruct((32, C, 128), F32),
        compiler_params=pltpu.CompilerParams(vmem_limit_bytes=20 << 20),
        cost_estimate=pl.CostEstimate(flops=2 * 2048 * 64 * 128, bytes_accessed=1 << 20, transcendentals=0),
        name="outer",
    )(spectrum, pair)


def gelu_slope(values):
    return (
        0.5 * (1.0 + lax.erf(values * ROOT_HALF))
        + values * jnp.exp(-0.5 * values * values) * ROOT_TWO_PI
    )


def block_diagonal(square):
    wide = jnp.concatenate([square, square], axis=1)
    full = jnp.concatenate([wide, wide], axis=0)
    return jnp.where(iota(full.shape, 0) // C == iota(full.shape, 1) // C, full, 0.0)


def inner_rows(core, scale, own_ref, other_ref, rows_ref):
    own = own_ref[:XC].astype(F32).reshape(XC * 32, 128)
    other = other_ref[:XC].astype(F32).reshape(XC * 32, 128)
    sign = parity(core, own.shape) * scale
    half_a = jnp.where(core == 0, own, other) * sign
    half_b = jnp.where(core == 0, other, own) * sign
    low = iota(own.shape, 1) < 64
    first = jnp.where(low, half_a, pltpu.roll(half_b, 64, 1)).reshape(XC * 4, 8, 128)
    second = jnp.where(low, pltpu.roll(half_a, 64, 1), half_b).reshape(XC * 4, 8, 128)
    rows_ref[...] = jnp.stack([first, second], axis=1).reshape(XC * C, 128).astype(BF)


def mixed_cells(diagonal, inner, cells, back, start):
    pieces = []
    for k in range(cells.shape[0] // 128):
        rows = inner[start + 128 * k : start + 128 * k + 128, :]
        left = jnp.concatenate([diagonal, rows], axis=1)
        right = jnp.concatenate([cells[128 * k : 128 * k + 128], back], axis=0)
        pieces.append(dot(left, right))
    return jnp.concatenate(pieces, axis=0)


def cells_kernel(
    place,
    field_ref,
    cotangent_ref,
    own_in_ref,
    other_in_ref,
    local_ref,
    forth_ref,
    back_ref,
    slope_ref,
    own_ref,
    other_ref,
    weight_ref,
    inner,
):
    diagonal = block_diagonal(local_ref[...].astype(F32)).T.astype(BF)
    inner_rows(place[1], INVERSE, own_in_ref, other_in_ref, inner)
    products = jnp.zeros((256, 256), F32)
    tiles = [(half, y, g) for half in range(2) for y in range(YC // YB) for g in range(4)]
    flipped, ready, made = {}, {}, {}
    sums = {}

    def place_of(tile):
        half, y, g = tile
        cells = slice(16 * half + 4 * g, 16 * half + 4 * g + 4)
        return cells, slice(C * cells.start, C * cells.stop), slice(YB * y, YB * y + YB)

    def begin(tile):
        half, y, g = tile
        cells, rows, columns = place_of(tile)
        if g == 0:
            flipped[half, y] = jnp.swapaxes(cotangent_ref[:, 16 * half : 16 * half + 16, columns], 0, 1)
        field = field_ref[cells, :, columns].reshape(256, YB)
        ready[tile] = mixed_cells(diagonal, inner, field, back_ref[:, columns], rows.start)

    def bend(tile):
        half, y, g = tile
        cells, rows, columns = place_of(tile)
        upper = flipped[half, y][4 * g : 4 * g + 4].reshape(256, YB).astype(F32)
        slope = (upper * gelu_slope(ready.pop(tile))).astype(BF)
        slope_ref[cells, :, columns] = slope.reshape(4, C, YB)
        made[tile] = slope

    def end(tile, products):
        half, y, g = tile
        cells, rows, columns = place_of(tile)
        slope = made.pop(tile)
        field = field_ref[cells, :, columns].reshape(256, YB)
        part = dot(slope, forth_ref[columns, :])
        sums[half, g] = part if y == 0 else sums[half, g] + part
        return products + dot(field, slope, ((1,), (1,)))

    for t in range(len(tiles) + 2):
        if t < len(tiles):
            begin(tiles[t])
        if t >= 2:
            products = end(tiles[t - 2], products)
        if 1 <= t <= len(tiles):
            bend(tiles[t - 1])
    for half in range(2):
        cells = slice(16 * half, 16 * half + 16)
        parts = jnp.concatenate([sums[half, g] for g in range(4)], axis=0)
        own_ref[cells], other_ref[cells] = split_halves(parts, 16, 4, place[1])
    total = products[:64, :128] + pltpu.roll(products[64:128, :128], 64, 1)
    total = total + products[128:192, 128:] + pltpu.roll(products[192:, 128:], 64, 1)
    high = total.astype(BF).astype(F32)
    low = pltpu.roll(total - high, 64, 1)
    weight_ref[...] = jnp.where(iota((64, 128), 1) < 64, high, low).astype(BF)


def cells_step(place, cells, cotangent, own, other, local_weight, forth, back):
    return pl.pallas_call(
        cells_kernel,
        in_specs=[SMEM] + [VMEM] * 7,
        out_specs=[VMEM] * 4,
        out_shape=[
            pltpu.VMEM((XC, C, YC), BF),
            pltpu.VMEM((XC, 32, 128), BF),
            pltpu.VMEM((XC, 32, 128), BF),
            pltpu.VMEM((64, 128), BF),
        ],
        scratch_shapes=[pltpu.VMEM((XC * C, 128), BF)],
        compiler_params=pltpu.CompilerParams(vmem_limit_bytes=24 << 20),
        name="cells_step",
    )(place, cells, cotangent, own, other, local_weight, forth, back)


def last_kernel(
    place,
    slope_ref,
    own_in_ref,
    other_in_ref,
    local_ref,
    back_ref,
    out_ref,
    grad_local_ref,
    inner,
    staged,
    sent,
):
    total = own_in_ref[XC:].astype(F32).reshape(64, 128)
    total = total + pltpu.roll(total, 64, 1)
    more = other_in_ref[XC:].astype(F32).reshape(64, 128)
    more = more + pltpu.roll(more, 64, 1)
    grad_local_ref[...] = (total + more)[:, :64] * FORWARD
    diagonal = block_diagonal(local_ref[...].astype(F32)).astype(BF)
    inner_rows(place[1], FORWARD, own_in_ref, other_in_ref, inner)
    chunks = [(half, y) for half in range(2) for y in range(YC // YO)]

    def copy(k):
        half, y = chunks[k]
        target = out_ref.at[:, 16 * half : 16 * half + 16, YO * y : YO * y + YO]
        return pltpu.make_async_copy(staged.at[k], target, sent.at[k])

    def finish(k, pieces):
        staged[k] = jnp.swapaxes(jnp.concatenate(pieces, axis=0), 0, 1)
        copy(k).start()

    ready = None
    for k, (half, y) in enumerate(chunks):
        columns = slice(YO * y, YO * y + YO)
        pieces = []
        for g in range(4):
            cells = slice(16 * half + 4 * g, 16 * half + 4 * g + 4)
            slope = slope_ref[cells, :, columns].reshape(256, YO)
            total = mixed_cells(diagonal, inner, slope, back_ref[:, columns], C * cells.start)
            pieces.append(total.astype(BF).reshape(4, C, YO))
            if g == 0 and ready is not None:
                finish(k - 1, ready)
        ready = pieces
    finish(len(chunks) - 1, ready)
    for k in range(len(chunks)):
        copy(k).wait()


def last_step(place, slope, own, other, local_weight, back):
    number = 2 * (YC // YO)
    return pl.pallas_call(
        last_kernel,
        in_specs=[SMEM] + [VMEM] * 5,
        out_specs=[pl.BlockSpec(memory_space=pltpu.HBM), VMEM],
        scratch_shapes=[
            pltpu.VMEM((XC * C, 128), BF),
            pltpu.VMEM((number, C, 16, YO), BF),
            pltpu.SemaphoreType.DMA((number,)),
        ],
        out_shape=[
            jax.ShapeDtypeStruct((C, XC, YC), BF),
            jax.ShapeDtypeStruct((C, C), F32),
        ],
        compiler_params=pltpu.CompilerParams(vmem_limit_bytes=24 << 20),
        name="last_step",
    )(place, slope, own, other, local_weight, back)


def swap_cores(values):
    return lax.ppermute(values, "gy", [(0, 1), (1, 0)])


def exchange(rows):
    return lax.all_to_all(rows, "gx", 0, 0, tiled=True)


def on_device(field, cotangent, local_weight, spectral_weight):
    forth, back, phase, origin = tables()
    forth, back = [jnp.asarray(t.astype(np.float32), BF) for t in (forth, back)]
    phase_back = jnp.asarray(np.transpose(phase, (0, 2, 1)), F32)
    phase, origin = [jnp.asarray(t, F32) for t in (phase, origin)]
    place = jnp.stack([lax.axis_index("gx"), lax.axis_index("gy")]).astype(jnp.int32)
    weights = spectral_weight[0]

    cells, own, other = y_forward(place, field[0], forth)
    sent = exchange(x_forward(place, phase, origin, own, swap_cores(other), FORWARD))
    copies, spectrum = mix(sent, weights)
    inner = x_inverse(place, phase_back, origin, exchange(copies))
    slope, own, other, rider = cells_step(
        place, cells, cotangent[0], inner, swap_cores(inner), local_weight, forth, back
    )
    sent = exchange(x_forward(place, phase, origin, own, swap_cores(other), INVERSE, rider))
    copies, pair = mix_back(sent, weights)
    inner = x_inverse(place, phase_back, origin, exchange(copies))
    grad_spectral = outer(spectrum, pair)
    grad_field, grad_local = last_step(place, slope, inner, swap_cores(inner), local_weight, back)
    return (grad_field[None], grad_spectral[None], grad_local)


def solution(mesh):
    placed = (P(None, None, "gx", "gy"), P(None, None, "gx", "gy"), P(), P("gx", "gy", None, None))
    return jax.shard_map(
        on_device,
        mesh=mesh,
        in_specs=placed,
        out_specs=(P(None, None, "gx", "gy"), P("gx", "gy", None, None), P()),
        check_vma=False,
    )
```

```python
import math

import jax
import jax.experimental.pallas as pl
import jax.experimental.pallas.tpu as pltpu
import jax.numpy as jnp
import numpy as np
from jax import lax
from jax.sharding import PartitionSpec as P

NX = 2048
NY = 2048
C = 64
MX = 64
MY = 64
SHARDS = 64
XC = 32
YC = 1024
YB = 256
YO = 512
TWO_PI = 2.0 * math.pi
ROOT_HALF = 1.0 / math.sqrt(2.0)
ROOT_TWO_PI = 1.0 / math.sqrt(2.0 * math.pi)
FORWARD = 1.0 / math.sqrt(NX * NY)
INVERSE = 1.0 / math.sqrt(MX * MY)
GAMMA = math.sqrt(MX * MY / (NX * NY))
BF = jnp.bfloat16
F32 = jnp.float32
RIDER = 8


def tables():
    angle = (np.arange(YC)[:, None] * np.arange(MY)[None, :] % NY) * (TWO_PI / NY)
    pair = np.stack([np.cos(angle), -np.sin(angle)], axis=1).reshape(YC, 2, 2, 32)
    forth = np.transpose(pair, (0, 2, 1, 3)).reshape(YC, 128)
    modes = np.arange(MX)
    frequency = np.where(modes < MX // 2, modes, modes + NX - MX)
    xangle = (frequency[:, None] * np.arange(XC)[None, :] % NX) * (TWO_PI / NX)
    phase = np.stack([np.cos(xangle), np.sin(xangle)])
    origin = (modes[:, None] * np.arange(SHARDS)[None, :] % SHARDS) * (TWO_PI / SHARDS)
    packed = np.zeros((2, 160, 128))
    packed[:, :64, :XC] = phase
    packed[:, 64:96, :MX] = np.transpose(phase, (0, 2, 1))
    packed[:, 96:, :SHARDS] = np.stack([np.cos(origin), np.sin(origin)])
    return forth, forth.T, packed


def dot(a, b, dims=((1,), (0,))):
    return lax.dot_general(a, b, (dims, ((), ())), preferred_element_type=F32)


VMEM = pl.BlockSpec(memory_space=pltpu.VMEM)
SMEM = pl.BlockSpec(memory_space=pltpu.SMEM)


def iota(shape, axis):
    return lax.broadcasted_iota(jnp.int32, shape, axis)


def turn(values, sign):
    lane = iota(values.shape, 1)
    first = lane % 64 < 32
    return jnp.where(first, sign * pltpu.roll(values, 96, 1), -sign * pltpu.roll(values, 32, 1))


def parity(core, shape):
    return jnp.where((iota(shape, len(shape) - 1) % 2) * core == 1, -1.0, 1.0).astype(F32)


def split_halves(parts, cells, groups, core):
    rows = cells * groups * 8
    blocks = parts.reshape(cells * groups, 2, 8, 128)
    first = blocks[:, 0].reshape(rows, 128)
    second = blocks[:, 1].reshape(rows, 128)
    low = iota((rows, 128), 1) < 64
    sign = parity(core, (rows, 128))
    half_a = jnp.where(low, first, pltpu.roll(second, 64, 1)) * sign
    half_b = jnp.where(low, pltpu.roll(first, 64, 1), second) * sign
    own = jnp.where(core == 0, half_a, half_b)
    other = jnp.where(core == 0, half_b, half_a)
    shape = (cells, groups * 8, 128)
    return own.reshape(shape).astype(BF), other.reshape(shape).astype(BF)


def rotated(phase_ref, shard, rows, columns, axis):
    at = iota((MX, SHARDS), 1 - axis) == shard
    cosine, sine = [
        jnp.sum(jnp.where(at, phase_ref[q, 96:, :SHARDS], 0.0), axis=1 - axis, keepdims=True) for q in range(2)
    ]
    real, imag = [phase_ref[q, rows, :columns] for q in range(2)]
    return (cosine * real - sine * imag).astype(BF), (sine * real + cosine * imag).astype(BF)


def x_matrices(phase_ref, shard):
    widen = (iota((XC, 256), 1) // 8 == iota((XC, 256), 0)).astype(BF)
    keep = iota((1, 8, 256), 2) % 8 == iota((1, 8, 256), 1)
    forward = []
    for table in rotated(phase_ref, shard, slice(0, 64), XC, 0):
        wide = dot(table, widen)
        forward.append(jnp.where(keep, wide[:, None, :], 0.0).reshape(512, 256).astype(BF))
    widen = (iota((MX, 512), 1) // 8 == iota((MX, 512), 0)).astype(BF)
    keep = iota((1, 8, 512), 2) % 8 == iota((1, 8, 512), 1)
    inverse = []
    for table in rotated(phase_ref, shard, slice(64, 96), MX, 1):
        wide = dot(table, widen)
        inverse.append(jnp.where(keep, wide[:, None, :], 0.0).reshape(256, 512).astype(BF))
    return jnp.concatenate(forward, axis=1), jnp.concatenate(inverse, axis=0)


def y_forward_kernel(
    place,
    field_ref,
    table_ref,
    phase_ref,
    cells_ref,
    own_ref,
    other_ref,
    forth_ref,
    forward_ref,
    inverse_ref,
    held,
    phase,
    arrived,
):
    def copy(k):
        group, half = k // 2, k % 2
        channels = pl.ds(pl.multiple_of(32 * group, 32), 32)
        cells = pl.ds(pl.multiple_of(16 * half, 16), 16)
        return pltpu.make_async_copy(field_ref.at[channels, cells], held.at[k], arrived.at[k])

    copy_phase = pltpu.make_async_copy(phase_ref, phase, arrived.at[4])
    copy_table = pltpu.make_async_copy(table_ref, forth_ref, arrived.at[5])
    copy_phase.start()
    copy_table.start()
    for k in range(4):
        copy(k).start()
    copy_phase.wait()
    forward_ref[...], inverse_ref[...] = x_matrices(phase, place[0])
    copy_table.wait()

    @pl.loop(0, 4)
    def _(k):
        group, half = k // 2, k % 2
        copy(k).wait()
        rows = jnp.swapaxes(held[k], 0, 1)
        cells = pl.ds(pl.multiple_of(16 * half, 16), 16)
        cells_ref[cells, pl.ds(pl.multiple_of(32 * group, 32), 32), :] = rows
        parts = dot(rows.reshape(16 * 32, YC), forth_ref[...])
        own, other = split_halves(parts, 16, 2, place[1])
        channels = pl.ds(pl.multiple_of(16 * group, 16), 16)
        own_ref[cells, channels, :] = own
        other_ref[cells, channels, :] = other


def y_forward(place, field, forth, phase):
    away = pl.BlockSpec(memory_space=pltpu.HBM)
    operands = [pltpu.with_memory_space_constraint(a, pltpu.HBM) for a in (field, forth, phase)]
    return pl.pallas_call(
        y_forward_kernel,
        in_specs=[SMEM, away, away, away],
        out_specs=[VMEM] * 6,
        out_shape=[
            pltpu.VMEM((XC, C, YC), BF),
            pltpu.VMEM((XC, 32, 128), BF),
            pltpu.VMEM((XC, 32, 128), BF),
            pltpu.VMEM((YC, 128), BF),
            pltpu.VMEM((512, 512), BF),
            pltpu.VMEM((512, 512), BF),
        ],
        scratch_shapes=[
            pltpu.VMEM((4, 32, 16, YC), BF),
            pltpu.VMEM((2, 160, 128), F32),
            pltpu.SemaphoreType.DMA((6,)),
        ],
        compiler_params=pltpu.CompilerParams(vmem_limit_bytes=16 << 20),
        name="y_forward",
    )(place, *operands)


def x_forward_kernel(scale, left_ref, own_ref, other_ref, *rest):
    out_ref = rest[-1]
    total = own_ref[...].astype(F32) + other_ref[...].astype(F32)
    left = left_ref[...]
    for g in range(2):
        right = []
        for s in range(2):
            rows = total[:, 16 * g + 8 * s : 16 * g + 8 * s + 8].reshape(256, 128)
            right.append(jnp.concatenate([rows, turn(rows, 1.0)], axis=0))
        modes = dot(left, jnp.concatenate(right, axis=1).astype(BF)) * scale
        both = [modes[:, 128 * s : 128 * s + 128].reshape(64, 8, 128) for s in range(2)]
        out_ref[:, 16 * g : 16 * g + 16, :] = jnp.concatenate(both, axis=1).astype(BF)
    if len(rest) == 2:
        rider = rest[0][...].astype(F32)
        out_ref[:, 32:, :] = jnp.broadcast_to(rider[:, None, :], (64, RIDER, 128)).astype(BF)


def x_forward(left, own, other, scale, rider=None):
    rows = 32 if rider is None else 32 + RIDER
    operands = [own, other] + ([] if rider is None else [rider])
    return pl.pallas_call(
        lambda *refs: x_forward_kernel(scale, *refs),
        in_specs=[VMEM] * (1 + len(operands)),
        out_specs=VMEM,
        out_shape=pltpu.VMEM((SHARDS, rows, 128), BF),
        compiler_params=pltpu.CompilerParams(vmem_limit_bytes=16 << 20),
        name="x_forward",
    )(left, *operands)


def x_inverse_kernel(left_ref, sent_ref, inner_ref):
    left = left_ref[...]
    for g in range(2):
        rows = sent_ref[:, 16 * g : 16 * g + 16, :].astype(F32)
        right = [rows[:, 8 * s : 8 * s + 8].reshape(512, 128) for s in range(2)]
        both = dot(left, jnp.concatenate(right, axis=1).astype(BF))
        inner = []
        for s in range(2):
            piece = both[:, 128 * s : 128 * s + 128]
            inner.append((piece[:256] + turn(piece[256:], -1.0)).reshape(XC, 8, 128))
        inner_ref[:XC, 16 * g : 16 * g + 16, :] = jnp.concatenate(inner, axis=1).astype(BF)
    if sent_ref.shape[1] > 32:
        rider = sent_ref[:, 32:, :].astype(F32)[:, 0, :]
        inner_ref[XC:, :, :] = rider.reshape(2, 32, 128).astype(BF)


def x_inverse(left, sent):
    cells = XC if sent.shape[1] == 32 else XC + 2
    return pl.pallas_call(
        x_inverse_kernel,
        in_specs=[VMEM, VMEM],
        out_specs=VMEM,
        out_shape=pltpu.VMEM((cells, 32, 128), BF),
        compiler_params=pltpu.CompilerParams(vmem_limit_bytes=16 << 20),
        name="x_inverse",
    )(left, sent)


def pick(b):
    r = iota((32, C), 0)
    return (iota((32, C), 1) == (r // 8) * 16 + b * 8 + r % 8).astype(BF)


def modes_of(rows):
    flipped = rows.T.astype(BF)
    return (dot(flipped[:64], pick(0)) + dot(flipped[64:], pick(1))).astype(BF)


def rows_of(real, imag):
    blocks = [dot(pick(b), part, ((1,), (1,))) for b in range(2) for part in (real, imag)]
    return jnp.concatenate(blocks, axis=1)


def own_mode(shape):
    return iota(shape, 1) // C == iota(shape, 0) % 32


def mix_kernel(sent_ref, weight_ref, out_ref, spectrum_ref):
    spectrum = modes_of(jnp.sum(sent_ref[...].astype(F32), axis=0))
    spectrum_ref[...] = spectrum
    pair = spectrum.astype(F32)
    pair = jnp.concatenate([pair, pair], axis=1)
    wide = jnp.concatenate([pair] * 16, axis=1)
    wide = jnp.where(own_mode(wide.shape), wide, 0.0).astype(BF)
    product = dot(wide, weight_ref[...].reshape(32 * C, 128))
    lane = iota((32, 128), 1)
    mixed = product[:32] + jnp.where(lane < 64, -1.0, 1.0) * pltpu.roll(product[32:], 64, 1)
    mixed = mixed.astype(BF)
    rows = rows_of(mixed[:, :64], mixed[:, 64:])
    out_ref[...] = jnp.broadcast_to(rows[None], (SHARDS, 32, 128)).astype(BF)


def mix(sent, weights):
    return pl.pallas_call(
        mix_kernel,
        out_shape=[
            jax.ShapeDtypeStruct((SHARDS, 32, 128), BF),
            jax.ShapeDtypeStruct((64, C), BF),
        ],
        compiler_params=pltpu.CompilerParams(vmem_limit_bytes=20 << 20),
        name="mix",
    )(sent, weights)


def mix_back_kernel(sent_ref, weight_ref, out_ref, pair_ref):
    total = jnp.sum(sent_ref[...].astype(F32), axis=0)
    modes = modes_of(total[:32]).astype(F32)
    real, imag = modes[:32], modes[32:]
    left = jnp.concatenate([real, imag], axis=1)
    right = jnp.concatenate([imag, -real], axis=1)
    pair = jnp.concatenate([left, right], axis=0).astype(BF)
    pair_ref[...] = pair
    product = dot(pair, weight_ref[...].reshape(32 * C, 128), ((1,), (1,)))
    product = jnp.where(own_mode(product.shape), product, 0.0)
    folded = product[:, :128]
    for k in range(1, 16):
        folded = folded + product[:, 128 * k : 128 * k + 128]
    folded = (folded + pltpu.roll(folded, 64, 1))[:, :64].astype(BF)
    rows = rows_of(folded[:32], folded[32:])
    rider = total[32:]
    rider = rider + pltpu.roll(rider, 64, 1)
    high = rider.astype(BF).astype(F32)
    rider = jnp.where(iota(rider.shape, 1) < 64, high, rider - high)
    rows = jnp.concatenate([rows, rider], axis=0)
    out_ref[...] = jnp.broadcast_to(rows[None], (SHARDS, 32 + RIDER, 128)).astype(BF)


def mix_back(sent, weights):
    return pl.pallas_call(
        mix_back_kernel,
        out_shape=[
            jax.ShapeDtypeStruct((SHARDS, 32 + RIDER, 128), BF),
            jax.ShapeDtypeStruct((64, 128), BF),
        ],
        compiler_params=pltpu.CompilerParams(vmem_limit_bytes=20 << 20),
        name="mix_back",
    )(sent, weights)


def outer_kernel(spectrum_ref, pair_ref, out_ref, staged, sent):
    flipped = spectrum_ref[...].astype(F32).T
    tall = jnp.concatenate([flipped] * 16, axis=0)

    def copy(k):
        piece = slice(16 * k, 16 * k + 16)
        return pltpu.make_async_copy(staged.at[piece], out_ref.at[piece], sent.at[k])

    for k in range(2):
        keep = iota(tall.shape, 1) % 32 == iota(tall.shape, 0) // C + 16 * k
        rows = jnp.where(keep, tall, 0.0).astype(BF)
        staged[16 * k : 16 * k + 16] = (dot(rows, pair_ref[...]) * GAMMA).reshape(16, C, 128)
        copy(k).start()
    for k in range(2):
        copy(k).wait()


def outer(spectrum, pair):
    return pl.pallas_call(
        outer_kernel,
        in_specs=[VMEM, VMEM],
        out_specs=pl.BlockSpec(memory_space=pltpu.HBM),
        out_shape=jax.ShapeDtypeStruct((32, C, 128), F32),
        scratch_shapes=[pltpu.VMEM((32, C, 128), F32), pltpu.SemaphoreType.DMA((2,))],
        compiler_params=pltpu.CompilerParams(vmem_limit_bytes=16 << 20),
        cost_estimate=pl.CostEstimate(flops=1 << 30, bytes_accessed=1 << 20, transcendentals=0),
        name="outer",
    )(spectrum, pair)


def relaid_kernel(cells_ref, after_ref, out_ref):
    out_ref[...] = jnp.swapaxes(cells_ref[...], 0, 1)


def relaid(cells, after):
    return pl.pallas_call(
        relaid_kernel,
        in_specs=[VMEM, pl.BlockSpec(memory_space=pl.ANY)],
        out_specs=VMEM,
        out_shape=pltpu.VMEM((XC, C, YC), BF),
        compiler_params=pltpu.CompilerParams(vmem_limit_bytes=16 << 20),
        cost_estimate=pl.CostEstimate(flops=1 << 30, bytes_accessed=8 << 20, transcendentals=0),
        name="relaid",
    )(cells, after)


def weight_kernel(field_ref, slope_ref, weight_ref):
    products = jnp.zeros((256, 256), F32)
    for g in range(XC // 4):
        field = field_ref[4 * g : 4 * g + 4].reshape(256, YC)
        slope = slope_ref[4 * g : 4 * g + 4].reshape(256, YC)
        products = products + dot(field, slope, ((1,), (1,)))
    total = products[:64, :128] + pltpu.roll(products[64:128, :128], 64, 1)
    total = total + products[128:192, 128:] + pltpu.roll(products[192:, 128:], 64, 1)
    high = total.astype(BF).astype(F32)
    low = pltpu.roll(total - high, 64, 1)
    weight_ref[...] = jnp.where(iota((64, 128), 1) < 64, high, low).astype(BF)


def weight_step(cells, slope):
    return pl.pallas_call(
        weight_kernel,
        in_specs=[VMEM, VMEM],
        out_specs=VMEM,
        out_shape=pltpu.VMEM((64, 128), BF),
        compiler_params=pltpu.CompilerParams(vmem_limit_bytes=16 << 20),
        cost_estimate=pl.CostEstimate(flops=1 << 30, bytes_accessed=8 << 20, transcendentals=0),
        name="weight_step",
    )(cells, slope)


def gelu_slope(values):
    return (
        0.5 * (1.0 + lax.erf(values * ROOT_HALF))
        + values * jnp.exp(-0.5 * values * values) * ROOT_TWO_PI
    )


def block_diagonal(square):
    wide = jnp.concatenate([square, square], axis=1)
    full = jnp.concatenate([wide, wide], axis=0)
    return jnp.where(iota(full.shape, 0) // C == iota(full.shape, 1) // C, full, 0.0)


def inner_rows(core, scale, own_ref, other_ref, rows_ref):
    own = own_ref[:XC].astype(F32).reshape(XC * 32, 128)
    other = other_ref[:XC].astype(F32).reshape(XC * 32, 128)
    sign = parity(core, own.shape) * scale
    half_a = jnp.where(core == 0, own, other) * sign
    half_b = jnp.where(core == 0, other, own) * sign
    low = iota(own.shape, 1) < 64
    first = jnp.where(low, half_a, pltpu.roll(half_b, 64, 1)).reshape(XC * 4, 8, 128)
    second = jnp.where(low, pltpu.roll(half_a, 64, 1), half_b).reshape(XC * 4, 8, 128)
    rows_ref[...] = jnp.stack([first, second], axis=1).reshape(XC * C, 128).astype(BF)


def mixed_cells(diagonal, inner, cells, back, start):
    pieces = []
    for k in range(cells.shape[0] // 128):
        rows = inner[start + 128 * k : start + 128 * k + 128, :]
        left = jnp.concatenate([diagonal, rows], axis=1)
        right = jnp.concatenate([cells[128 * k : 128 * k + 128], back], axis=0)
        pieces.append(dot(left, right))
    return jnp.concatenate(pieces, axis=0)


def cells_kernel(
    place,
    field_ref,
    cotangent_ref,
    own_in_ref,
    other_in_ref,
    local_ref,
    forth_ref,
    back_ref,
    slope_ref,
    own_ref,
    other_ref,
    inner,
):
    diagonal = block_diagonal(local_ref[...].astype(F32)).T.astype(BF)
    inner_rows(place[1], INVERSE, own_in_ref, other_in_ref, inner)
    tiles = [(half, y, g) for half in range(2) for y in range(YC // YB) for g in range(4)]
    ready, made = {}, {}
    sums = {}

    def place_of(tile):
        half, y, g = tile
        cells = slice(16 * half + 4 * g, 16 * half + 4 * g + 4)
        return cells, slice(C * cells.start, C * cells.stop), slice(YB * y, YB * y + YB)

    def begin(tile):
        half, y, g = tile
        cells, rows, columns = place_of(tile)
        field = field_ref[cells, :, columns].reshape(256, YB)
        ready[tile] = mixed_cells(diagonal, inner, field, back_ref[:, columns], rows.start)

    def bend(tile):
        half, y, g = tile
        cells, rows, columns = place_of(tile)
        upper = cotangent_ref[cells, :, columns].reshape(256, YB).astype(F32)
        slope = (upper * gelu_slope(ready.pop(tile))).astype(BF)
        slope_ref[cells, :, columns] = slope.reshape(4, C, YB)
        made[tile] = slope

    def end(tile):
        half, y, g = tile
        cells, rows, columns = place_of(tile)
        slope = made.pop(tile)
        part = dot(slope, forth_ref[columns, :])
        sums[half, g] = part if y == 0 else sums[half, g] + part

    for t in range(len(tiles) + 2):
        if t < len(tiles):
            begin(tiles[t])
        if t >= 2:
            end(tiles[t - 2])
        if 1 <= t <= len(tiles):
            bend(tiles[t - 1])
    for half in range(2):
        cells = slice(16 * half, 16 * half + 16)
        parts = jnp.concatenate([sums[half, g] for g in range(4)], axis=0)
        own_ref[cells], other_ref[cells] = split_halves(parts, 16, 4, place[1])


def cells_step(place, cells, cotangent, own, other, local_weight, forth, back):
    return pl.pallas_call(
        cells_kernel,
        in_specs=[SMEM] + [VMEM] * 7,
        out_specs=[VMEM] * 3,
        out_shape=[
            pltpu.VMEM((XC, C, YC), BF),
            pltpu.VMEM((XC, 32, 128), BF),
            pltpu.VMEM((XC, 32, 128), BF),
        ],
        scratch_shapes=[pltpu.VMEM((XC * C, 128), BF)],
        compiler_params=pltpu.CompilerParams(vmem_limit_bytes=24 << 20),
        name="cells_step",
    )(place, cells, cotangent, own, other, local_weight, forth, back)


def last_kernel(
    place,
    slope_ref,
    own_in_ref,
    other_in_ref,
    local_ref,
    back_ref,
    out_ref,
    grad_local_ref,
    inner,
    staged,
    sent,
):
    total = own_in_ref[XC:].astype(F32).reshape(64, 128)
    total = total + pltpu.roll(total, 64, 1)
    more = other_in_ref[XC:].astype(F32).reshape(64, 128)
    more = more + pltpu.roll(more, 64, 1)
    grad_local_ref[...] = (total + more)[:, :64] * FORWARD
    diagonal = block_diagonal(local_ref[...].astype(F32)).astype(BF)
    inner_rows(place[1], FORWARD, own_in_ref, other_in_ref, inner)
    chunks = [(half, y) for half in range(2) for y in range(YC // YO)]

    def copy(k):
        half, y = chunks[k]
        target = out_ref.at[:, 16 * half : 16 * half + 16, YO * y : YO * y + YO]
        return pltpu.make_async_copy(staged.at[k], target, sent.at[k])

    def finish(k, pieces):
        staged[k] = jnp.swapaxes(jnp.concatenate(pieces, axis=0), 0, 1)
        copy(k).start()

    ready = None
    for k, (half, y) in enumerate(chunks):
        columns = slice(YO * y, YO * y + YO)
        pieces = []
        for g in range(4):
            cells = slice(16 * half + 4 * g, 16 * half + 4 * g + 4)
            slope = slope_ref[cells, :, columns].reshape(256, YO)
            total = mixed_cells(diagonal, inner, slope, back_ref[:, columns], C * cells.start)
            pieces.append(total.astype(BF).reshape(4, C, YO))
            if g == 0 and ready is not None:
                finish(k - 1, ready)
        ready = pieces
    finish(len(chunks) - 1, ready)
    for k in range(len(chunks)):
        copy(k).wait()


def last_step(place, slope, own, other, local_weight, back):
    number = 2 * (YC // YO)
    return pl.pallas_call(
        last_kernel,
        in_specs=[SMEM] + [VMEM] * 5,
        out_specs=[pl.BlockSpec(memory_space=pltpu.HBM), VMEM],
        scratch_shapes=[
            pltpu.VMEM((XC * C, 128), BF),
            pltpu.VMEM((number, C, 16, YO), BF),
            pltpu.SemaphoreType.DMA((number,)),
        ],
        out_shape=[
            jax.ShapeDtypeStruct((C, XC, YC), BF),
            jax.ShapeDtypeStruct((C, C), F32),
        ],
        compiler_params=pltpu.CompilerParams(vmem_limit_bytes=24 << 20),
        name="last_step",
    )(place, slope, own, other, local_weight, back)


def swap_cores(values):
    return lax.ppermute(values, "gy", [(0, 1), (1, 0)])


def exchange(rows):
    return lax.all_to_all(rows, "gx", 0, 0, tiled=True)


def on_device(field, cotangent, local_weight, spectral_weight):
    forth, back, phase = tables()
    forth, back = [jnp.asarray(t.astype(np.float32), BF) for t in (forth, back)]
    phase = jnp.asarray(phase, F32)
    place = jnp.stack([lax.axis_index("gx"), lax.axis_index("gy")]).astype(jnp.int32)
    weights = spectral_weight[0]

    cells, own, other, forth, forward, inverse = y_forward(place, field[0], forth, phase)
    sent = exchange(x_forward(forward, own, swap_cores(other), FORWARD))
    copies, spectrum = mix(sent, weights)
    inner = x_inverse(inverse, exchange(copies))
    other = swap_cores(inner)
    upper = relaid(cotangent[0], inner)
    slope, own, other = cells_step(place, cells, upper, inner, other, local_weight, forth, back)
    other = swap_cores(other)
    rider = weight_step(cells, slope)
    sent = exchange(x_forward(forward, own, other, INVERSE, rider))
    copies, pair = mix_back(sent, weights)
    inner = x_inverse(inverse, exchange(copies))
    other = swap_cores(inner)
    grad_spectral = outer(spectrum, pair)
    grad_field, grad_local = last_step(place, slope, inner, other, local_weight, back)
    return (grad_field[None], grad_spectral[None], grad_local)


def solution(mesh):
    placed = (P(None, None, "gx", "gy"), P(None, None, "gx", "gy"), P(), P("gx", "gy", None, None))
    return jax.shard_map(
        on_device,
        mesh=mesh,
        in_specs=placed,
        out_specs=(P(None, None, "gx", "gy"), P("gx", "gy", None, None), P()),
        check_vma=False,
    )
```

```python
import math

import jax
import jax.experimental.pallas as pl
import jax.experimental.pallas.tpu as pltpu
import jax.numpy as jnp
import numpy as np
from jax import lax
from jax.sharding import PartitionSpec as P

NX = 2048
NY = 2048
C = 64
MX = 64
MY = 64
SHARDS = 64
XC = 32
YC = 1024
YB = 256
YO = 512
TWO_PI = 2.0 * math.pi
ROOT_HALF = 1.0 / math.sqrt(2.0)
ROOT_TWO_PI = 1.0 / math.sqrt(2.0 * math.pi)
FORWARD = 1.0 / math.sqrt(NX * NY)
INVERSE = 1.0 / math.sqrt(MX * MY)
GAMMA = math.sqrt(MX * MY / (NX * NY))
BF = jnp.bfloat16
F32 = jnp.float32
RIDER = 8


def tables():
    angle = (np.arange(YC)[:, None] * np.arange(MY)[None, :] % NY) * (TWO_PI / NY)
    pair = np.stack([np.cos(angle), -np.sin(angle)], axis=1).reshape(YC, 2, 2, 32)
    forth = np.transpose(pair, (0, 2, 1, 3)).reshape(YC, 128)
    modes = np.arange(MX)
    frequency = np.where(modes < MX // 2, modes, modes + NX - MX)
    xangle = (frequency[:, None] * np.arange(XC)[None, :] % NX) * (TWO_PI / NX)
    phase = np.stack([np.cos(xangle), np.sin(xangle)])
    origin = (modes[:, None] * np.arange(SHARDS)[None, :] % SHARDS) * (TWO_PI / SHARDS)
    packed = np.zeros((2, 160, 128))
    packed[:, :64, :XC] = phase
    packed[:, 64:96, :MX] = np.transpose(phase, (0, 2, 1))
    packed[:, 96:, :SHARDS] = np.stack([np.cos(origin), np.sin(origin)])
    return forth, forth.T, packed


def dot(a, b, dims=((1,), (0,))):
    return lax.dot_general(a, b, (dims, ((), ())), preferred_element_type=F32)


VMEM = pl.BlockSpec(memory_space=pltpu.VMEM)
SMEM = pl.BlockSpec(memory_space=pltpu.SMEM)


def iota(shape, axis):
    return lax.broadcasted_iota(jnp.int32, shape, axis)


def turn(values, sign):
    lane = iota(values.shape, 1)
    first = lane % 64 < 32
    return jnp.where(first, sign * pltpu.roll(values, 96, 1), -sign * pltpu.roll(values, 32, 1))


def parity(core, shape):
    return jnp.where((iota(shape, len(shape) - 1) % 2) * core == 1, -1.0, 1.0).astype(F32)


def split_halves(parts, cells, groups, core):
    rows = cells * groups * 8
    blocks = parts.reshape(cells * groups, 2, 8, 128)
    first = blocks[:, 0].reshape(rows, 128)
    second = blocks[:, 1].reshape(rows, 128)
    low = iota((rows, 128), 1) < 64
    sign = parity(core, (rows, 128))
    half_a = jnp.where(low, first, pltpu.roll(second, 64, 1)) * sign
    half_b = jnp.where(low, pltpu.roll(first, 64, 1), second) * sign
    own = jnp.where(core == 0, half_a, half_b)
    other = jnp.where(core == 0, half_b, half_a)
    shape = (cells, groups * 8, 128)
    return own.reshape(shape).astype(BF), other.reshape(shape).astype(BF)


def rotated(phase_ref, shard, rows, columns, axis):
    at = iota((MX, SHARDS), 1 - axis) == shard
    cosine, sine = [
        jnp.sum(jnp.where(at, phase_ref[q, 96:, :SHARDS], 0.0), axis=1 - axis, keepdims=True) for q in range(2)
    ]
    real, imag = [phase_ref[q, rows, :columns] for q in range(2)]
    return (cosine * real - sine * imag).astype(BF), (sine * real + cosine * imag).astype(BF)


def x_matrices(phase_ref, shard):
    widen = (iota((XC, 256), 1) // 8 == iota((XC, 256), 0)).astype(BF)
    keep = iota((1, 8, 256), 2) % 8 == iota((1, 8, 256), 1)
    forward = []
    for table in rotated(phase_ref, shard, slice(0, 64), XC, 0):
        wide = dot(table, widen)
        forward.append(jnp.where(keep, wide[:, None, :], 0.0).reshape(512, 256).astype(BF))
    widen = (iota((MX, 512), 1) // 8 == iota((MX, 512), 0)).astype(BF)
    keep = iota((1, 8, 512), 2) % 8 == iota((1, 8, 512), 1)
    inverse = []
    for table in rotated(phase_ref, shard, slice(64, 96), MX, 1):
        wide = dot(table, widen)
        inverse.append(jnp.where(keep, wide[:, None, :], 0.0).reshape(256, 512).astype(BF))
    return jnp.concatenate(forward, axis=1), jnp.concatenate(inverse, axis=0)


def y_forward_kernel(
    place,
    field_ref,
    table_ref,
    phase_ref,
    cells_ref,
    own_ref,
    other_ref,
    forth_ref,
    forward_ref,
    inverse_ref,
    held,
    phase,
    arrived,
):
    def copy(k):
        group, half = k // 2, k % 2
        channels = pl.ds(pl.multiple_of(32 * group, 32), 32)
        cells = pl.ds(pl.multiple_of(16 * half, 16), 16)
        return pltpu.make_async_copy(field_ref.at[channels, cells], held.at[k], arrived.at[k])

    copy_phase = pltpu.make_async_copy(phase_ref, phase, arrived.at[4])
    copy_table = pltpu.make_async_copy(table_ref, forth_ref, arrived.at[5])
    copy_phase.start()
    copy_table.start()
    for k in range(4):
        copy(k).start()
    copy_phase.wait()
    forward_ref[...], inverse_ref[...] = x_matrices(phase, place[0])
    copy_table.wait()

    @pl.loop(0, 4)
    def _(k):
        group, half = k // 2, k % 2
        copy(k).wait()
        rows = jnp.swapaxes(held[k], 0, 1)
        cells = pl.ds(pl.multiple_of(16 * half, 16), 16)
        cells_ref[cells, pl.ds(pl.multiple_of(32 * group, 32), 32), :] = rows
        parts = dot(rows.reshape(16 * 32, YC), forth_ref[...])
        own, other = split_halves(parts, 16, 2, place[1])
        channels = pl.ds(pl.multiple_of(16 * group, 16), 16)
        own_ref[cells, channels, :] = own
        other_ref[cells, channels, :] = other


def y_forward(place, field, forth, phase):
    away = pl.BlockSpec(memory_space=pltpu.HBM)
    operands = [pltpu.with_memory_space_constraint(a, pltpu.HBM) for a in (field, forth, phase)]
    return pl.pallas_call(
        y_forward_kernel,
        in_specs=[SMEM, away, away, away],
        out_specs=[VMEM] * 6,
        out_shape=[
            pltpu.VMEM((XC, C, YC), BF),
            pltpu.VMEM((XC, 32, 128), BF),
            pltpu.VMEM((XC, 32, 128), BF),
            pltpu.VMEM((YC, 128), BF),
            pltpu.VMEM((512, 512), BF),
            pltpu.VMEM((512, 512), BF),
        ],
        scratch_shapes=[
            pltpu.VMEM((4, 32, 16, YC), BF),
            pltpu.VMEM((2, 160, 128), F32),
            pltpu.SemaphoreType.DMA((6,)),
        ],
        compiler_params=pltpu.CompilerParams(vmem_limit_bytes=16 << 20),
        name="y_forward",
    )(place, *operands)


def x_forward_kernel(scale, left_ref, own_ref, other_ref, *rest):
    out_ref = rest[-1]
    total = own_ref[...].astype(F32) + other_ref[...].astype(F32)
    left = left_ref[...]
    for g in range(2):
        right = []
        for s in range(2):
            rows = total[:, 16 * g + 8 * s : 16 * g + 8 * s + 8].reshape(256, 128)
            right.append(jnp.concatenate([rows, turn(rows, 1.0)], axis=0))
        modes = dot(left, jnp.concatenate(right, axis=1).astype(BF)) * scale
        both = [modes[:, 128 * s : 128 * s + 128].reshape(64, 8, 128) for s in range(2)]
        out_ref[:, 16 * g : 16 * g + 16, :] = jnp.concatenate(both, axis=1).astype(BF)
    if len(rest) == 2:
        rider = rest[0][...].astype(F32)
        out_ref[:, 32:, :] = jnp.broadcast_to(rider[:, None, :], (64, RIDER, 128)).astype(BF)


def x_forward(left, own, other, scale, rider=None):
    rows = 32 if rider is None else 32 + RIDER
    operands = [own, other] + ([] if rider is None else [rider])
    return pl.pallas_call(
        lambda *refs: x_forward_kernel(scale, *refs),
        in_specs=[VMEM] * (1 + len(operands)),
        out_specs=VMEM,
        out_shape=pltpu.VMEM((SHARDS, rows, 128), BF),
        compiler_params=pltpu.CompilerParams(vmem_limit_bytes=16 << 20),
        name="x_forward",
    )(left, *operands)


def x_inverse_kernel(left_ref, sent_ref, inner_ref):
    left = left_ref[...]
    for g in range(2):
        rows = sent_ref[:, 16 * g : 16 * g + 16, :].astype(F32)
        right = [rows[:, 8 * s : 8 * s + 8].reshape(512, 128) for s in range(2)]
        both = dot(left, jnp.concatenate(right, axis=1).astype(BF))
        inner = []
        for s in range(2):
            piece = both[:, 128 * s : 128 * s + 128]
            inner.append((piece[:256] + turn(piece[256:], -1.0)).reshape(XC, 8, 128))
        inner_ref[:XC, 16 * g : 16 * g + 16, :] = jnp.concatenate(inner, axis=1).astype(BF)
    if sent_ref.shape[1] > 32:
        rider = sent_ref[:, 32:, :].astype(F32)[:, 0, :]
        inner_ref[XC:, :, :] = rider.reshape(2, 32, 128).astype(BF)


def x_inverse(left, sent):
    cells = XC if sent.shape[1] == 32 else XC + 2
    return pl.pallas_call(
        x_inverse_kernel,
        in_specs=[VMEM, VMEM],
        out_specs=VMEM,
        out_shape=pltpu.VMEM((cells, 32, 128), BF),
        compiler_params=pltpu.CompilerParams(vmem_limit_bytes=16 << 20),
        name="x_inverse",
    )(left, sent)


def pick(b):
    r = iota((32, C), 0)
    return (iota((32, C), 1) == (r // 8) * 16 + b * 8 + r % 8).astype(BF)


def modes_of(rows):
    flipped = rows.T.astype(BF)
    return (dot(flipped[:64], pick(0)) + dot(flipped[64:], pick(1))).astype(BF)


def rows_of(real, imag):
    blocks = [dot(pick(b), part, ((1,), (1,))) for b in range(2) for part in (real, imag)]
    return jnp.concatenate(blocks, axis=1)


def own_mode(shape):
    return iota(shape, 1) // C == iota(shape, 0) % 32


def mix_kernel(sent_ref, weight_ref, out_ref, spectrum_ref):
    spectrum = modes_of(jnp.sum(sent_ref[...].astype(F32), axis=0))
    spectrum_ref[...] = spectrum
    pair = spectrum.astype(F32)
    pair = jnp.concatenate([pair, pair], axis=1)
    wide = jnp.concatenate([pair] * 16, axis=1)
    wide = jnp.where(own_mode(wide.shape), wide, 0.0).astype(BF)
    product = dot(wide, weight_ref[...].reshape(32 * C, 128))
    lane = iota((32, 128), 1)
    mixed = product[:32] + jnp.where(lane < 64, -1.0, 1.0) * pltpu.roll(product[32:], 64, 1)
    mixed = mixed.astype(BF)
    rows = rows_of(mixed[:, :64], mixed[:, 64:])
    out_ref[...] = jnp.broadcast_to(rows[None], (SHARDS, 32, 128)).astype(BF)


def mix(sent, weights):
    return pl.pallas_call(
        mix_kernel,
        out_shape=[
            jax.ShapeDtypeStruct((SHARDS, 32, 128), BF),
            jax.ShapeDtypeStruct((64, C), BF),
        ],
        compiler_params=pltpu.CompilerParams(vmem_limit_bytes=20 << 20),
        name="mix",
    )(sent, weights)


def mix_back_kernel(sent_ref, weight_ref, out_ref, pair_ref):
    total = jnp.sum(sent_ref[...].astype(F32), axis=0)
    modes = modes_of(total[:32]).astype(F32)
    real, imag = modes[:32], modes[32:]
    left = jnp.concatenate([real, imag], axis=1)
    right = jnp.concatenate([imag, -real], axis=1)
    pair = jnp.concatenate([left, right], axis=0).astype(BF)
    pair_ref[...] = pair
    product = dot(pair, weight_ref[...].reshape(32 * C, 128), ((1,), (1,)))
    product = jnp.where(own_mode(product.shape), product, 0.0)
    folded = product[:, :128]
    for k in range(1, 16):
        folded = folded + product[:, 128 * k : 128 * k + 128]
    folded = (folded + pltpu.roll(folded, 64, 1))[:, :64].astype(BF)
    rows = rows_of(folded[:32], folded[32:])
    rider = total[32:]
    rider = rider + pltpu.roll(rider, 64, 1)
    high = rider.astype(BF).astype(F32)
    rider = jnp.where(iota(rider.shape, 1) < 64, high, rider - high)
    rows = jnp.concatenate([rows, rider], axis=0)
    out_ref[...] = jnp.broadcast_to(rows[None], (SHARDS, 32 + RIDER, 128)).astype(BF)


def mix_back(sent, weights):
    return pl.pallas_call(
        mix_back_kernel,
        out_shape=[
            jax.ShapeDtypeStruct((SHARDS, 32 + RIDER, 128), BF),
            jax.ShapeDtypeStruct((64, 128), BF),
        ],
        compiler_params=pltpu.CompilerParams(vmem_limit_bytes=20 << 20),
        name="mix_back",
    )(sent, weights)


def outer_kernel(spectrum_ref, pair_ref, out_ref, staged, sent):
    flipped = spectrum_ref[...].astype(F32).T
    tall = jnp.concatenate([flipped] * 16, axis=0)

    def copy(k):
        piece = slice(16 * k, 16 * k + 16)
        return pltpu.make_async_copy(staged.at[piece], out_ref.at[piece], sent.at[k])

    for k in range(2):
        keep = iota(tall.shape, 1) % 32 == iota(tall.shape, 0) // C + 16 * k
        rows = jnp.where(keep, tall, 0.0).astype(BF)
        staged[16 * k : 16 * k + 16] = (dot(rows, pair_ref[...]) * GAMMA).reshape(16, C, 128)
        copy(k).start()
    for k in range(2):
        copy(k).wait()


def outer(spectrum, pair):
    return pl.pallas_call(
        outer_kernel,
        in_specs=[VMEM, VMEM],
        out_specs=pl.BlockSpec(memory_space=pltpu.HBM),
        out_shape=jax.ShapeDtypeStruct((32, C, 128), F32),
        scratch_shapes=[pltpu.VMEM((32, C, 128), F32), pltpu.SemaphoreType.DMA((2,))],
        compiler_params=pltpu.CompilerParams(vmem_limit_bytes=16 << 20),
        cost_estimate=pl.CostEstimate(flops=1 << 30, bytes_accessed=1 << 20, transcendentals=0),
        name="outer",
    )(spectrum, pair)


def relaid_kernel(cells_ref, after_ref, out_ref):
    out_ref[...] = jnp.swapaxes(cells_ref[...] * jnp.asarray(0.5, BF), 0, 1)


def relaid(cells, after):
    return pl.pallas_call(
        relaid_kernel,
        in_specs=[VMEM, pl.BlockSpec(memory_space=pl.ANY)],
        out_specs=VMEM,
        out_shape=pltpu.VMEM((XC, C, YC), BF),
        compiler_params=pltpu.CompilerParams(vmem_limit_bytes=16 << 20),
        cost_estimate=pl.CostEstimate(flops=1 << 30, bytes_accessed=8 << 20, transcendentals=0),
        name="relaid",
    )(cells, after)


def weight_kernel(field_ref, slope_ref, weight_ref):
    products = jnp.zeros((256, 256), F32)
    for g in range(XC // 4):
        field = field_ref[4 * g : 4 * g + 4].reshape(256, YC)
        slope = slope_ref[4 * g : 4 * g + 4].reshape(256, YC)
        products = products + dot(field, slope, ((1,), (1,)))
    total = products[:64, :128] + pltpu.roll(products[64:128, :128], 64, 1)
    total = total + products[128:192, 128:] + pltpu.roll(products[192:, 128:], 64, 1)
    high = total.astype(BF).astype(F32)
    low = pltpu.roll(total - high, 64, 1)
    weight_ref[...] = jnp.where(iota((64, 128), 1) < 64, high, low).astype(BF)


def weight_step(cells, slope):
    return pl.pallas_call(
        weight_kernel,
        in_specs=[VMEM, VMEM],
        out_specs=VMEM,
        out_shape=pltpu.VMEM((64, 128), BF),
        compiler_params=pltpu.CompilerParams(vmem_limit_bytes=16 << 20),
        cost_estimate=pl.CostEstimate(flops=1 << 30, bytes_accessed=8 << 20, transcendentals=0),
        name="weight_step",
    )(cells, slope)


def gelu_slope(values):
    bell = jnp.exp2(values * values * (-0.5 / math.log(2.0)))
    return (1.0 + lax.erf(values * ROOT_HALF)) + (values * (2.0 * ROOT_TWO_PI)) * bell


def block_diagonal(square):
    wide = jnp.concatenate([square, square], axis=1)
    full = jnp.concatenate([wide, wide], axis=0)
    return jnp.where(iota(full.shape, 0) // C == iota(full.shape, 1) // C, full, 0.0)


def inner_rows(core, scale, own_ref, other_ref, rows_ref):
    own = own_ref[:XC].astype(F32).reshape(XC * 32, 128)
    other = other_ref[:XC].astype(F32).reshape(XC * 32, 128)
    sign = parity(core, own.shape) * scale
    half_a = jnp.where(core == 0, own, other) * sign
    half_b = jnp.where(core == 0, other, own) * sign
    low = iota(own.shape, 1) < 64
    first = jnp.where(low, half_a, pltpu.roll(half_b, 64, 1)).reshape(XC * 4, 8, 128)
    second = jnp.where(low, pltpu.roll(half_a, 64, 1), half_b).reshape(XC * 4, 8, 128)
    rows_ref[...] = jnp.stack([first, second], axis=1).reshape(XC * C, 128).astype(BF)


def mixed_cells(diagonal, inner, cells, back, start):
    pieces = []
    for k in range(cells.shape[0] // 128):
        rows = inner[start + 128 * k : start + 128 * k + 128, :]
        left = jnp.concatenate([diagonal, rows], axis=1)
        right = jnp.concatenate([cells[128 * k : 128 * k + 128], back], axis=0)
        pieces.append(dot(left, right))
    return jnp.concatenate(pieces, axis=0)


def cells_kernel(
    place,
    field_ref,
    cotangent_ref,
    own_in_ref,
    other_in_ref,
    local_ref,
    forth_ref,
    back_ref,
    slope_ref,
    own_ref,
    other_ref,
    inner,
):
    diagonal = block_diagonal(local_ref[...].astype(F32)).T.astype(BF)
    inner_rows(place[1], INVERSE, own_in_ref, other_in_ref, inner)
    tiles = [(half, y, g) for half in range(2) for y in range(YC // YB) for g in range(4)]
    ready, made = {}, {}
    sums = {}

    def place_of(tile):
        half, y, g = tile
        cells = slice(16 * half + 4 * g, 16 * half + 4 * g + 4)
        return cells, slice(C * cells.start, C * cells.stop), slice(YB * y, YB * y + YB)

    def begin(tile):
        half, y, g = tile
        cells, rows, columns = place_of(tile)
        field = field_ref[cells, :, columns].reshape(256, YB)
        ready[tile] = mixed_cells(diagonal, inner, field, back_ref[:, columns], rows.start)

    def bend(tile):
        half, y, g = tile
        cells, rows, columns = place_of(tile)
        upper = cotangent_ref[cells, :, columns].reshape(256, YB).astype(F32)
        slope = (upper * gelu_slope(ready.pop(tile))).astype(BF)
        slope_ref[cells, :, columns] = slope.reshape(4, C, YB)
        made[tile] = slope

    def end(tile):
        half, y, g = tile
        cells, rows, columns = place_of(tile)
        slope = made.pop(tile)
        part = dot(slope, forth_ref[columns, :])
        sums[half, g] = part if y == 0 else sums[half, g] + part

    for t in range(len(tiles) + 2):
        if t < len(tiles):
            begin(tiles[t])
        if t >= 2:
            end(tiles[t - 2])
        if 1 <= t <= len(tiles):
            bend(tiles[t - 1])
    for half in range(2):
        cells = slice(16 * half, 16 * half + 16)
        parts = jnp.concatenate([sums[half, g] for g in range(4)], axis=0)
        own_ref[cells], other_ref[cells] = split_halves(parts, 16, 4, place[1])


def cells_step(place, cells, cotangent, own, other, local_weight, forth, back):
    return pl.pallas_call(
        cells_kernel,
        in_specs=[SMEM] + [VMEM] * 7,
        out_specs=[VMEM] * 3,
        out_shape=[
            pltpu.VMEM((XC, C, YC), BF),
            pltpu.VMEM((XC, 32, 128), BF),
            pltpu.VMEM((XC, 32, 128), BF),
        ],
        scratch_shapes=[pltpu.VMEM((XC * C, 128), BF)],
        compiler_params=pltpu.CompilerParams(vmem_limit_bytes=24 << 20),
        name="cells_step",
    )(place, cells, cotangent, own, other, local_weight, forth, back)


def last_kernel(
    place,
    slope_ref,
    own_in_ref,
    other_in_ref,
    local_ref,
    back_ref,
    out_ref,
    grad_local_ref,
    inner,
    staged,
    sent,
):
    total = own_in_ref[XC:].astype(F32).reshape(64, 128)
    total = total + pltpu.roll(total, 64, 1)
    more = other_in_ref[XC:].astype(F32).reshape(64, 128)
    more = more + pltpu.roll(more, 64, 1)
    grad_local_ref[...] = (total + more)[:, :64] * FORWARD
    diagonal = block_diagonal(local_ref[...].astype(F32)).astype(BF)
    inner_rows(place[1], FORWARD, own_in_ref, other_in_ref, inner)
    chunks = [(half, y) for half in range(2) for y in range(YC // YO)]

    def copy(k):
        half, y = chunks[k]
        target = out_ref.at[:, 16 * half : 16 * half + 16, YO * y : YO * y + YO]
        return pltpu.make_async_copy(staged.at[k], target, sent.at[k])

    def finish(k, pieces):
        staged[k] = jnp.swapaxes(jnp.concatenate(pieces, axis=0), 0, 1)
        copy(k).start()

    ready = None
    for k, (half, y) in enumerate(chunks):
        columns = slice(YO * y, YO * y + YO)
        pieces = []
        for g in range(4):
            cells = slice(16 * half + 4 * g, 16 * half + 4 * g + 4)
            slope = slope_ref[cells, :, columns].reshape(256, YO)
            total = mixed_cells(diagonal, inner, slope, back_ref[:, columns], C * cells.start)
            pieces.append(total.astype(BF).reshape(4, C, YO))
            if g == 0 and ready is not None:
                finish(k - 1, ready)
        ready = pieces
    finish(len(chunks) - 1, ready)
    for k in range(len(chunks)):
        copy(k).wait()


def last_step(place, slope, own, other, local_weight, back):
    number = 2 * (YC // YO)
    return pl.pallas_call(
        last_kernel,
        in_specs=[SMEM] + [VMEM] * 5,
        out_specs=[pl.BlockSpec(memory_space=pltpu.HBM), VMEM],
        scratch_shapes=[
            pltpu.VMEM((XC * C, 128), BF),
            pltpu.VMEM((number, C, 16, YO), BF),
            pltpu.SemaphoreType.DMA((number,)),
        ],
        out_shape=[
            jax.ShapeDtypeStruct((C, XC, YC), BF),
            jax.ShapeDtypeStruct((C, C), F32),
        ],
        compiler_params=pltpu.CompilerParams(vmem_limit_bytes=24 << 20),
        name="last_step",
    )(place, slope, own, other, local_weight, back)


def swap_cores(values):
    return lax.ppermute(values, "gy", [(0, 1), (1, 0)])


def exchange(rows):
    return lax.all_to_all(rows, "gx", 0, 0, tiled=True)


def on_device(field, cotangent, local_weight, spectral_weight):
    forth, back, phase = tables()
    forth, back = [jnp.asarray(t.astype(np.float32), BF) for t in (forth, back)]
    phase = jnp.asarray(phase, F32)
    place = jnp.stack([lax.axis_index("gx"), lax.axis_index("gy")]).astype(jnp.int32)
    weights = spectral_weight[0]

    cells, own, other, forth, forward, inverse = y_forward(place, field[0], forth, phase)
    sent = exchange(x_forward(forward, own, swap_cores(other), FORWARD))
    copies, spectrum = mix(sent, weights)
    inner = x_inverse(inverse, exchange(copies))
    other = swap_cores(inner)
    upper = relaid(cotangent[0], inner)
    slope, own, other = cells_step(place, cells, upper, inner, other, local_weight, forth, back)
    other = swap_cores(other)
    rider = weight_step(cells, slope)
    sent = exchange(x_forward(forward, own, other, INVERSE, rider))
    copies, pair = mix_back(sent, weights)
    inner = x_inverse(inverse, exchange(copies))
    other = swap_cores(inner)
    grad_spectral = outer(spectrum, pair)
    grad_field, grad_local = last_step(place, slope, inner, other, local_weight, back)
    return (grad_field[None], grad_spectral[None], grad_local)


def solution(mesh):
    placed = (P(None, None, "gx", "gy"), P(None, None, "gx", "gy"), P(), P("gx", "gy", None, None))
    return jax.shard_map(
        on_device,
        mesh=mesh,
        in_specs=placed,
        out_specs=(P(None, None, "gx", "gy"), P("gx", "gy", None, None), P()),
        check_vma=False,
    )
```

```python
import math

import jax
import jax.experimental.pallas as pl
import jax.experimental.pallas.tpu as pltpu
import jax.numpy as jnp
import numpy as np
from jax import lax
from jax.sharding import PartitionSpec as P

NX = 2048
NY = 2048
C = 64
MX = 64
MY = 64
SHARDS = 64
XC = 32
YC = 1024
YB = 256
YO = 512
TWO_PI = 2.0 * math.pi
ROOT_HALF = 1.0 / math.sqrt(2.0)
ROOT_TWO_PI = 1.0 / math.sqrt(2.0 * math.pi)
FORWARD = 1.0 / math.sqrt(NX * NY)
INVERSE = 1.0 / math.sqrt(MX * MY)
GAMMA = math.sqrt(MX * MY / (NX * NY))
BF = jnp.bfloat16
F32 = jnp.float32
RIDER = 8


def tables():
    angle = (np.arange(YC)[:, None] * np.arange(MY)[None, :] % NY) * (TWO_PI / NY)
    pair = np.stack([np.cos(angle), -np.sin(angle)], axis=1).reshape(YC, 2, 2, 32)
    forth = np.transpose(pair, (0, 2, 1, 3)).reshape(YC, 128)
    modes = np.arange(MX)
    frequency = np.where(modes < MX // 2, modes, modes + NX - MX)
    xangle = (frequency[:, None] * np.arange(XC)[None, :] % NX) * (TWO_PI / NX)
    phase = np.stack([np.cos(xangle), np.sin(xangle)])
    origin = (modes[:, None] * np.arange(SHARDS)[None, :] % SHARDS) * (TWO_PI / SHARDS)
    packed = np.zeros((2, 160, 128))
    packed[:, :64, :XC] = phase
    packed[:, 64:96, :MX] = np.transpose(phase, (0, 2, 1))
    packed[:, 96:, :SHARDS] = np.stack([np.cos(origin), np.sin(origin)])
    return forth, forth.T, packed


def dot(a, b, dims=((1,), (0,))):
    return lax.dot_general(a, b, (dims, ((), ())), preferred_element_type=F32)


VMEM = pl.BlockSpec(memory_space=pltpu.VMEM)
SMEM = pl.BlockSpec(memory_space=pltpu.SMEM)


def iota(shape, axis):
    return lax.broadcasted_iota(jnp.int32, shape, axis)


def turn(values, sign):
    lane = iota(values.shape, 1)
    first = lane % 64 < 32
    return jnp.where(first, sign * pltpu.roll(values, 96, 1), -sign * pltpu.roll(values, 32, 1))


def parity(core, shape):
    return jnp.where((iota(shape, len(shape) - 1) % 2) * core == 1, -1.0, 1.0).astype(F32)


def split_halves(parts, cells, groups, core):
    rows = cells * groups * 8
    blocks = parts.reshape(cells * groups, 2, 8, 128)
    first = blocks[:, 0].reshape(rows, 128)
    second = blocks[:, 1].reshape(rows, 128)
    low = iota((rows, 128), 1) < 64
    sign = parity(core, (rows, 128))
    half_a = jnp.where(low, first, pltpu.roll(second, 64, 1)) * sign
    half_b = jnp.where(low, pltpu.roll(first, 64, 1), second) * sign
    own = jnp.where(core == 0, half_a, half_b)
    other = jnp.where(core == 0, half_b, half_a)
    shape = (cells, groups * 8, 128)
    return own.reshape(shape), other.reshape(shape)


def rotated(phase_ref, shard, rows, columns, axis):
    at = iota((MX, SHARDS), 1 - axis) == shard
    cosine, sine = [
        jnp.sum(jnp.where(at, phase_ref[q, 96:, :SHARDS], 0.0), axis=1 - axis, keepdims=True) for q in range(2)
    ]
    real, imag = [phase_ref[q, rows, :columns] for q in range(2)]
    return (cosine * real - sine * imag).astype(BF), (sine * real + cosine * imag).astype(BF)


def x_matrices(phase_ref, shard):
    widen = (iota((XC, 256), 1) // 8 == iota((XC, 256), 0)).astype(BF)
    keep = iota((1, 8, 256), 2) % 8 == iota((1, 8, 256), 1)
    forward = []
    for table in rotated(phase_ref, shard, slice(0, 64), XC, 0):
        wide = dot(table, widen)
        forward.append(jnp.where(keep, wide[:, None, :], 0.0).reshape(512, 256).astype(BF))
    widen = (iota((MX, 512), 1) // 8 == iota((MX, 512), 0)).astype(BF)
    keep = iota((1, 8, 512), 2) % 8 == iota((1, 8, 512), 1)
    inverse = []
    for table in rotated(phase_ref, shard, slice(64, 96), MX, 1):
        wide = dot(table, widen)
        inverse.append(jnp.where(keep, wide[:, None, :], 0.0).reshape(256, 512).astype(BF))
    return jnp.concatenate(forward, axis=1), jnp.concatenate(inverse, axis=0)


def y_forward_kernel(
    place,
    field_ref,
    table_ref,
    phase_ref,
    cells_ref,
    own_ref,
    other_ref,
    forth_ref,
    forward_ref,
    inverse_ref,
    held,
    phase,
    kept,
    arrived,
):
    def copy(k):
        channels = pl.ds(pl.multiple_of(16 * k, 16), 16)
        return pltpu.make_async_copy(field_ref.at[channels], held.at[k], arrived.at[k])

    copy_phase = pltpu.make_async_copy(phase_ref, phase, arrived.at[4])
    copy_table = pltpu.make_async_copy(table_ref, forth_ref, arrived.at[5])
    copy_phase.start()
    copy_table.start()
    for k in range(4):
        copy(k).start()
    copy_phase.wait()
    forward_ref[...], inverse_ref[...] = x_matrices(phase, place[0])
    copy_table.wait()

    @pl.loop(0, 4)
    def _(k):
        copy(k).wait()
        rows = jnp.swapaxes(held[k], 0, 1)
        cells_ref[:, pl.ds(pl.multiple_of(16 * k, 16), 16), :] = rows
        parts = dot(rows.reshape(XC * 16, YC), forth_ref[...])
        own, other = split_halves(parts, XC, 1, place[1])
        kept[0, :, pl.ds(pl.multiple_of(8 * k, 8), 8), :] = own
        kept[1, :, pl.ds(pl.multiple_of(8 * k, 8), 8), :] = other

    other_ref[...] = kept[1].astype(BF)
    own_ref[...] = kept[0].astype(BF)


def y_forward(place, field, forth, phase):
    away = pl.BlockSpec(memory_space=pltpu.HBM)
    operands = [pltpu.with_memory_space_constraint(a, pltpu.HBM) for a in (field, forth, phase)]
    return pl.pallas_call(
        y_forward_kernel,
        in_specs=[SMEM, away, away, away],
        out_specs=[VMEM] * 6,
        out_shape=[
            pltpu.VMEM((XC, C, YC), BF),
            pltpu.VMEM((XC, 32, 128), BF),
            pltpu.VMEM((XC, 32, 128), BF),
            pltpu.VMEM((YC, 128), BF),
            pltpu.VMEM((512, 512), BF),
            pltpu.VMEM((512, 512), BF),
        ],
        scratch_shapes=[
            pltpu.VMEM((4, 16, XC, YC), BF),
            pltpu.VMEM((2, 160, 128), F32),
            pltpu.VMEM((2, XC, 32, 128), F32),
            pltpu.SemaphoreType.DMA((6,)),
        ],
        compiler_params=pltpu.CompilerParams(vmem_limit_bytes=16 << 20),
        name="y_forward",
    )(place, *operands)


def x_forward_kernel(scale, left_ref, own_ref, other_ref, *rest):
    out_ref = rest[-1]
    total = own_ref[...].astype(F32) + other_ref[...].astype(F32)
    left = left_ref[...]
    for g in range(2):
        right = []
        for s in range(2):
            rows = total[:, 16 * g + 8 * s : 16 * g + 8 * s + 8].reshape(256, 128)
            right.append(jnp.concatenate([rows, turn(rows, 1.0)], axis=0))
        modes = dot(left, jnp.concatenate(right, axis=1).astype(BF)) * scale
        both = [modes[:, 128 * s : 128 * s + 128].reshape(64, 8, 128) for s in range(2)]
        out_ref[:, 16 * g : 16 * g + 16, :] = jnp.concatenate(both, axis=1).astype(BF)
    if len(rest) == 2:
        rider = rest[0][...].astype(F32)
        out_ref[:, 32:, :] = jnp.broadcast_to(rider[:, None, :], (64, RIDER, 128)).astype(BF)


def x_forward(left, own, other, scale, rider=None):
    rows = 32 if rider is None else 32 + RIDER
    operands = [own, other] + ([] if rider is None else [rider])
    return pl.pallas_call(
        lambda *refs: x_forward_kernel(scale, *refs),
        in_specs=[VMEM] * (1 + len(operands)),
        out_specs=VMEM,
        out_shape=pltpu.VMEM((SHARDS, rows, 128), BF),
        compiler_params=pltpu.CompilerParams(vmem_limit_bytes=16 << 20),
        name="x_forward",
    )(left, *operands)


def x_inverse_kernel(left_ref, sent_ref, inner_ref):
    left = left_ref[...]
    for g in range(2):
        rows = sent_ref[:, 16 * g : 16 * g + 16, :].astype(F32)
        right = [rows[:, 8 * s : 8 * s + 8].reshape(512, 128) for s in range(2)]
        both = dot(left, jnp.concatenate(right, axis=1).astype(BF))
        inner = []
        for s in range(2):
            piece = both[:, 128 * s : 128 * s + 128]
            inner.append((piece[:256] + turn(piece[256:], -1.0)).reshape(XC, 8, 128))
        inner_ref[:XC, 16 * g : 16 * g + 16, :] = jnp.concatenate(inner, axis=1).astype(BF)
    if sent_ref.shape[1] > 32:
        rider = sent_ref[:, 32:, :].astype(F32)[:, 0, :]
        inner_ref[XC:, :, :] = rider.reshape(2, 32, 128).astype(BF)


def x_inverse(left, sent):
    cells = XC if sent.shape[1] == 32 else XC + 2
    return pl.pallas_call(
        x_inverse_kernel,
        in_specs=[VMEM, VMEM],
        out_specs=VMEM,
        out_shape=pltpu.VMEM((cells, 32, 128), BF),
        compiler_params=pltpu.CompilerParams(vmem_limit_bytes=16 << 20),
        name="x_inverse",
    )(left, sent)


def pick(b):
    r = iota((32, C), 0)
    return (iota((32, C), 1) == (r // 8) * 16 + b * 8 + r % 8).astype(BF)


def modes_of(rows):
    flipped = rows.T.astype(BF)
    return (dot(flipped[:64], pick(0)) + dot(flipped[64:], pick(1))).astype(BF)


def rows_of(real, imag):
    blocks = [dot(pick(b), part, ((1,), (1,))) for b in range(2) for part in (real, imag)]
    return jnp.concatenate(blocks, axis=1)


def summed(sent_ref):
    total = sent_ref[:8].astype(F32)
    for k in range(1, 8):
        total = total + sent_ref[8 * k : 8 * k + 8].astype(F32)
    total = total[:4] + total[4:]
    total = total[:2] + total[2:]
    return total[0] + total[1]


def own_mode(shape):
    return iota(shape, 1) // C == iota(shape, 0) % 32


def mix_kernel(sent_ref, weight_ref, out_ref, spectrum_ref):
    spectrum = modes_of(summed(sent_ref))
    spectrum_ref[...] = spectrum
    pair = spectrum.astype(F32)
    pair = jnp.concatenate([pair, pair], axis=1)
    wide = jnp.concatenate([pair] * 16, axis=1)
    wide = jnp.where(own_mode(wide.shape), wide, 0.0).astype(BF)
    product = dot(wide, weight_ref[...].reshape(32 * C, 128))
    lane = iota((32, 128), 1)
    mixed = product[:32] + jnp.where(lane < 64, -1.0, 1.0) * pltpu.roll(product[32:], 64, 1)
    mixed = mixed.astype(BF)
    rows = rows_of(mixed[:, :64], mixed[:, 64:])
    out_ref[...] = jnp.broadcast_to(rows[None], (SHARDS, 32, 128)).astype(BF)


def mix(sent, weights):
    return pl.pallas_call(
        mix_kernel,
        out_shape=[
            jax.ShapeDtypeStruct((SHARDS, 32, 128), BF),
            jax.ShapeDtypeStruct((64, C), BF),
        ],
        compiler_params=pltpu.CompilerParams(vmem_limit_bytes=20 << 20),
        name="mix",
    )(sent, weights)


def mix_back_kernel(sent_ref, weight_ref, out_ref, pair_ref):
    total = summed(sent_ref)
    modes = modes_of(total[:32]).astype(F32)
    real, imag = modes[:32], modes[32:]
    left = jnp.concatenate([real, imag], axis=1)
    right = jnp.concatenate([imag, -real], axis=1)
    pair = jnp.concatenate([left, right], axis=0).astype(BF)
    pair_ref[...] = pair
    product = dot(pair, weight_ref[...].reshape(32 * C, 128), ((1,), (1,)))
    product = jnp.where(own_mode(product.shape), product, 0.0)
    folded = product[:, :128]
    for k in range(1, 16):
        folded = folded + product[:, 128 * k : 128 * k + 128]
    folded = (folded + pltpu.roll(folded, 64, 1))[:, :64].astype(BF)
    rows = rows_of(folded[:32], folded[32:])
    rider = total[32:]
    rider = rider + pltpu.roll(rider, 64, 1)
    high = rider.astype(BF).astype(F32)
    rider = jnp.where(iota(rider.shape, 1) < 64, high, rider - high)
    rows = jnp.concatenate([rows, rider], axis=0)
    out_ref[...] = jnp.broadcast_to(rows[None], (SHARDS, 32 + RIDER, 128)).astype(BF)


def mix_back(sent, weights):
    return pl.pallas_call(
        mix_back_kernel,
        out_shape=[
            jax.ShapeDtypeStruct((SHARDS, 32 + RIDER, 128), BF),
            jax.ShapeDtypeStruct((64, 128), BF),
        ],
        compiler_params=pltpu.CompilerParams(vmem_limit_bytes=20 << 20),
        name="mix_back",
    )(sent, weights)


def outer_kernel(spectrum_ref, pair_ref, out_ref, staged, sent):
    flipped = spectrum_ref[...].astype(F32).T
    tall = jnp.concatenate([flipped] * 16, axis=0)

    def copy(k):
        piece = slice(16 * k, 16 * k + 16)
        return pltpu.make_async_copy(staged.at[piece], out_ref.at[piece], sent.at[k])

    for k in range(2):
        keep = iota(tall.shape, 1) % 32 == iota(tall.shape, 0) // C + 16 * k
        rows = jnp.where(keep, tall, 0.0).astype(BF)
        staged[16 * k : 16 * k + 16] = (dot(rows, pair_ref[...]) * GAMMA).reshape(16, C, 128)
        copy(k).start()
    for k in range(2):
        copy(k).wait()


def outer(spectrum, pair):
    return pl.pallas_call(
        outer_kernel,
        in_specs=[VMEM, VMEM],
        out_specs=pl.BlockSpec(memory_space=pltpu.HBM),
        out_shape=jax.ShapeDtypeStruct((32, C, 128), F32),
        scratch_shapes=[pltpu.VMEM((32, C, 128), F32), pltpu.SemaphoreType.DMA((2,))],
        compiler_params=pltpu.CompilerParams(vmem_limit_bytes=16 << 20),
        cost_estimate=pl.CostEstimate(flops=1 << 30, bytes_accessed=1 << 20, transcendentals=0),
        name="outer",
    )(spectrum, pair)


def relaid_kernel(cells_ref, after_ref, out_ref):
    out_ref[...] = jnp.swapaxes(cells_ref[...] * jnp.asarray(0.5, BF), 0, 1)


def relaid(cells, after):
    return pl.pallas_call(
        relaid_kernel,
        in_specs=[VMEM, pl.BlockSpec(memory_space=pl.ANY)],
        out_specs=VMEM,
        out_shape=pltpu.VMEM((XC, C, YC), BF),
        compiler_params=pltpu.CompilerParams(vmem_limit_bytes=16 << 20),
        cost_estimate=pl.CostEstimate(flops=1 << 30, bytes_accessed=8 << 20, transcendentals=0),
        name="relaid",
    )(cells, after)


def weight_kernel(field_ref, slope_ref, weight_ref):
    products = jnp.zeros((256, 256), F32)
    for g in range(XC // 4):
        field = field_ref[4 * g : 4 * g + 4].reshape(256, YC)
        slope = slope_ref[4 * g : 4 * g + 4].reshape(256, YC)
        products = products + dot(field, slope, ((1,), (1,)))
    total = products[:64, :128] + pltpu.roll(products[64:128, :128], 64, 1)
    total = total + products[128:192, 128:] + pltpu.roll(products[192:, 128:], 64, 1)
    high = total.astype(BF).astype(F32)
    low = pltpu.roll(total - high, 64, 1)
    weight_ref[...] = jnp.where(iota((64, 128), 1) < 64, high, low).astype(BF)


def weight_step(cells, slope):
    return pl.pallas_call(
        weight_kernel,
        in_specs=[VMEM, VMEM],
        out_specs=VMEM,
        out_shape=pltpu.VMEM((64, 128), BF),
        compiler_params=pltpu.CompilerParams(vmem_limit_bytes=16 << 20),
        cost_estimate=pl.CostEstimate(flops=1 << 30, bytes_accessed=8 << 20, transcendentals=0),
        name="weight_step",
    )(cells, slope)


def gelu_slope(values):
    bell = jnp.exp2(values * values * (-0.5 / math.log(2.0)))
    return (1.0 + lax.erf(values * ROOT_HALF)) + (values * (2.0 * ROOT_TWO_PI)) * bell


def block_diagonal(square):
    wide = jnp.concatenate([square, square], axis=1)
    full = jnp.concatenate([wide, wide], axis=0)
    return jnp.where(iota(full.shape, 0) // C == iota(full.shape, 1) // C, full, 0.0)


def inner_rows(core, scale, own_ref, other_ref, rows_ref):
    own = own_ref[:XC].astype(F32).reshape(XC * 32, 128)
    other = other_ref[:XC].astype(F32).reshape(XC * 32, 128)
    sign = parity(core, own.shape) * scale
    half_a = jnp.where(core == 0, own, other) * sign
    half_b = jnp.where(core == 0, other, own) * sign
    low = iota(own.shape, 1) < 64
    first = jnp.where(low, half_a, pltpu.roll(half_b, 64, 1)).reshape(XC * 4, 8, 128)
    second = jnp.where(low, pltpu.roll(half_a, 64, 1), half_b).reshape(XC * 4, 8, 128)
    rows_ref[...] = jnp.stack([first, second], axis=1).reshape(XC * C, 128).astype(BF)


def mixed_cells(diagonal, inner, cells, back, start):
    pieces = []
    for k in range(cells.shape[0] // 128):
        rows = inner[start + 128 * k : start + 128 * k + 128, :]
        left = jnp.concatenate([diagonal, rows], axis=1)
        right = jnp.concatenate([cells[128 * k : 128 * k + 128], back], axis=0)
        pieces.append(dot(left, right))
    return jnp.concatenate(pieces, axis=0)


def cells_kernel(
    place,
    field_ref,
    cotangent_ref,
    own_in_ref,
    other_in_ref,
    local_ref,
    forth_ref,
    back_ref,
    slope_ref,
    own_ref,
    other_ref,
    inner,
):
    diagonal = block_diagonal(local_ref[...].astype(F32)).T.astype(BF)
    inner_rows(place[1], INVERSE, own_in_ref, other_in_ref, inner)
    tiles = [(half, y, g) for half in range(2) for y in range(YC // YB) for g in range(4)]
    ready, made = {}, {}
    sums = {}

    def place_of(tile):
        half, y, g = tile
        cells = slice(16 * half + 4 * g, 16 * half + 4 * g + 4)
        return cells, slice(C * cells.start, C * cells.stop), slice(YB * y, YB * y + YB)

    def begin(tile):
        half, y, g = tile
        cells, rows, columns = place_of(tile)
        field = field_ref[cells, :, columns].reshape(256, YB)
        ready[tile] = mixed_cells(diagonal, inner, field, back_ref[:, columns], rows.start)

    def bend(tile):
        half, y, g = tile
        cells, rows, columns = place_of(tile)
        upper = cotangent_ref[cells, :, columns].reshape(256, YB).astype(F32)
        slope = (upper * gelu_slope(ready.pop(tile))).astype(BF)
        slope_ref[cells, :, columns] = slope.reshape(4, C, YB)
        made[tile] = slope

    def end(tile):
        half, y, g = tile
        cells, rows, columns = place_of(tile)
        slope = made.pop(tile)
        part = dot(slope, forth_ref[columns, :])
        sums[half, g] = part if y == 0 else sums[half, g] + part

    for t in range(len(tiles) + 2):
        if t < len(tiles):
            begin(tiles[t])
        if t >= 2:
            end(tiles[t - 2])
        if 1 <= t <= len(tiles):
            bend(tiles[t - 1])
    for half in range(2):
        cells = slice(16 * half, 16 * half + 16)
        parts = jnp.concatenate([sums[half, g] for g in range(4)], axis=0)
        own, other = split_halves(parts, 16, 4, place[1])
        own_ref[cells], other_ref[cells] = own.astype(BF), other.astype(BF)


def cells_step(place, cells, cotangent, own, other, local_weight, forth, back):
    return pl.pallas_call(
        cells_kernel,
        in_specs=[SMEM] + [VMEM] * 7,
        out_specs=[VMEM] * 3,
        out_shape=[
            pltpu.VMEM((XC, C, YC), BF),
            pltpu.VMEM((XC, 32, 128), BF),
            pltpu.VMEM((XC, 32, 128), BF),
        ],
        scratch_shapes=[pltpu.VMEM((XC * C, 128), BF)],
        compiler_params=pltpu.CompilerParams(vmem_limit_bytes=24 << 20),
        name="cells_step",
    )(place, cells, cotangent, own, other, local_weight, forth, back)


def last_kernel(
    place,
    slope_ref,
    own_in_ref,
    other_in_ref,
    local_ref,
    back_ref,
    out_ref,
    grad_local_ref,
    inner,
    staged,
    sent,
):
    total = own_in_ref[XC:].astype(F32).reshape(64, 128)
    total = total + pltpu.roll(total, 64, 1)
    more = other_in_ref[XC:].astype(F32).reshape(64, 128)
    more = more + pltpu.roll(more, 64, 1)
    grad_local_ref[...] = (total + more)[:, :64] * FORWARD
    diagonal = block_diagonal(local_ref[...].astype(F32)).astype(BF)
    inner_rows(place[1], FORWARD, own_in_ref, other_in_ref, inner)
    chunks = [(half, y) for half in range(2) for y in range(YC // YO)]

    def copy(k):
        half, y = chunks[k]
        target = out_ref.at[:, 16 * half : 16 * half + 16, YO * y : YO * y + YO]
        return pltpu.make_async_copy(staged.at[k], target, sent.at[k])

    def finish(k, pieces):
        staged[k] = jnp.swapaxes(jnp.concatenate(pieces, axis=0), 0, 1)
        copy(k).start()

    ready = None
    for k, (half, y) in enumerate(chunks):
        columns = slice(YO * y, YO * y + YO)
        pieces = []
        for g in range(4):
            cells = slice(16 * half + 4 * g, 16 * half + 4 * g + 4)
            slope = slope_ref[cells, :, columns].reshape(256, YO)
            total = mixed_cells(diagonal, inner, slope, back_ref[:, columns], C * cells.start)
            pieces.append(total.astype(BF).reshape(4, C, YO))
            if g == 0 and ready is not None:
                finish(k - 1, ready)
        ready = pieces
    finish(len(chunks) - 1, ready)
    for k in range(len(chunks)):
        copy(k).wait()


def last_step(place, slope, own, other, local_weight, back):
    number = 2 * (YC // YO)
    return pl.pallas_call(
        last_kernel,
        in_specs=[SMEM] + [VMEM] * 5,
        out_specs=[pl.BlockSpec(memory_space=pltpu.HBM), VMEM],
        scratch_shapes=[
            pltpu.VMEM((XC * C, 128), BF),
            pltpu.VMEM((number, C, 16, YO), BF),
            pltpu.SemaphoreType.DMA((number,)),
        ],
        out_shape=[
            jax.ShapeDtypeStruct((C, XC, YC), BF),
            jax.ShapeDtypeStruct((C, C), F32),
        ],
        compiler_params=pltpu.CompilerParams(vmem_limit_bytes=24 << 20),
        name="last_step",
    )(place, slope, own, other, local_weight, back)


def swap_cores(values):
    return lax.ppermute(values, "gy", [(0, 1), (1, 0)])


def exchange(rows):
    return lax.all_to_all(rows, "gx", 0, 0, tiled=True)


def on_device(field, cotangent, local_weight, spectral_weight):
    forth, back, phase = tables()
    forth, back = [jnp.asarray(t.astype(np.float32), BF) for t in (forth, back)]
    phase = jnp.asarray(phase, F32)
    place = jnp.stack([lax.axis_index("gx"), lax.axis_index("gy")]).astype(jnp.int32)
    weights = spectral_weight[0]

    cells, own, other, forth, forward, inverse = y_forward(place, field[0], forth, phase)
    sent = exchange(x_forward(forward, own, swap_cores(other), FORWARD))
    copies, spectrum = mix(sent, weights)
    inner = x_inverse(inverse, exchange(copies))
    other = swap_cores(inner)
    upper = relaid(cotangent[0], inner)
    slope, own, other = cells_step(place, cells, upper, inner, other, local_weight, forth, back)
    other = swap_cores(other)
    rider = weight_step(cells, slope)
    sent = exchange(x_forward(forward, own, other, INVERSE, rider))
    copies, pair = mix_back(sent, weights)
    inner = x_inverse(inverse, exchange(copies))
    other = swap_cores(inner)
    grad_spectral = outer(spectrum, pair)
    grad_field, grad_local = last_step(place, slope, inner, other, local_weight, back)
    return (grad_field[None], grad_spectral[None], grad_local)


def solution(mesh):
    placed = (P(None, None, "gx", "gy"), P(None, None, "gx", "gy"), P(), P("gx", "gy", None, None))
    return jax.shard_map(
        on_device,
        mesh=mesh,
        in_specs=placed,
        out_specs=(P(None, None, "gx", "gy"), P("gx", "gy", None, None), P()),
        check_vma=False,
    )
```
